256 devices in a mesh: space: 32 (over z_hi, x, core), port: 8 (over z_lo, y).
Axes of the slice: x: 4, y: 4, z: 8 (z_hi: 4, z_lo: 2; z = z_hi * 2 + z_lo), core: 2. Of those that a mesh axis runs over, the one named last changes fastest.
Arguments:
- fields: float32 [2, 8, 6, 128, 64, 128], P(None, 'port', None, 'space'), may hold values from -6 to 6
- inv_eps: float32 [3, 128, 64, 128], P(None, 'space'), may hold values from 0.04 to 0.48
- tensor_tiles: float32 [32, 32, 24, 128], P('space'), may hold values from -0.08 to 0.32
- tile_index: int32 [32, 32, 4], P('space'), may hold values from -1 to 255, as said below
- ports: int32 [2, 8], replicated, may hold values from 0 to 1048575
- waves: float32 [2, 8, 8], P(None, 'port'), may hold values from -8 to 8
Outputs:
- fields_out: float32 [2, 8, 6, 128, 64, 128], P(None, 'port', None, 'space')
- sensitivity: float32 [128, 64, 128], P('space', 'port')
The draws below stay inside these ranges and needn't reach their ends.
Inputs may be any that keep to these rules, and one draw needn't show every extreme that they name: tile_index[d, s, k] is -1 for an empty slot or a column number j of slab d (x-major); no number repeats within one slab's lists; the live slots of one owner come first; every owner has one or more live slots for every slab; slot 0 from owner 0 of every slab holds the column 255; some slab gets all 4 slots live from every owner.
All inputs are finite; a program needn't handle non-finite values.
Results may differ from the reference program's by a relative error of at most 0.0003.
Values sent between devices are 32-bit elements; how exact they have to be, the bound alone decides.
No kernel may reach another device: no remote copies, remote signals or barrier semaphores. Data moves between devices by JAX's collectives and lax.ppermute only.
A program may use at most 64 MiB of HBM per device.

```python
import math
import jax
import jax.numpy as jnp
from jax import lax

CX = 4
NY = 64
NZ = 128
STEPS = 8
CAP = 4
SLABS = 32
NX = 128
PORTS = 8


def draw_tensor_tiles(key, part):
    first, second, third = jax.random.split(key, 3)
    shape = (SLABS, SLABS, CAP, 6, NZ)
    entry = jnp.arange(6).reshape(1, 1, 1, 6, 1)
    diagonal = jax.random.uniform(first, shape, jnp.float32, 0.2, 0.3)
    magnitude = jax.random.uniform(second, shape, jnp.float32, 0.02, 0.08)
    signs = jnp.where(jax.random.bernoulli(third, 0.5, shape), 1.0, -1.0)
    values = jnp.where(entry < 3, diagonal, signs * magnitude)
    return values.reshape(SLABS, SLABS, CAP * 6, NZ).astype(jnp.float32)


def draw_tile_index(key, part):
    keys = jax.random.split(key, 5)
    heavy = jax.random.randint(keys[0], (SLABS,), 0, 2)
    light_count = jax.random.randint(keys[1], (SLABS, SLABS), 1, 3)
    heavy_count = jax.random.randint(keys[2], (SLABS, SLABS), 1, CAP + 1)
    counts = jnp.where(heavy[None, :] == 1, heavy_count, light_count)
    full_slab = jax.random.randint(keys[3], (), 0, SLABS)
    counts = jnp.where(jnp.arange(SLABS)[None, :] == full_slab, CAP, counts)
    counts = jnp.minimum(counts, CAP)
    offsets = jnp.cumsum(counts, axis=0) - counts
    column_total = CX * NY
    raw_orders = jax.vmap(lambda sub_key: jax.random.permutation(sub_key, column_total))(jax.random.split(keys[4], SLABS))
    orders = (raw_orders - raw_orders[:, :1] - 1) % column_total
    slot_ids = jnp.arange(CAP)[None, None, :]
    ranks = jnp.minimum(offsets[:, :, None] + slot_ids, column_total - 1)
    chosen = orders[jnp.arange(SLABS)[None, :, None], ranks]
    live = slot_ids < counts[:, :, None]
    result = jnp.where(live, chosen, -1)
    return result.transpose(1, 0, 2).astype(jnp.int32)


def plant(entries, key, low, high):
    longest = entries.shape.index(max(entries.shape))
    spots = []
    for shift in (0, 1):
        where = [jax.random.randint(jax.random.fold_in(key, axis), (), 0, length) for axis, length in enumerate(entries.shape)]
        where[longest] = (where[longest] + shift) % entries.shape[longest]
        spots.append(tuple(where))
    return entries.at[spots[0]].set(low).at[spots[1]].set(high)


def levels(rng, extent, cuts, low, high):
    gain, own = 1.0, jax.random.fold_in(rng, 6)
    for position, parts in cuts:
        steps = jnp.exp(jax.random.uniform(jax.random.fold_in(own, position), (parts,), jnp.float32, low / len(cuts), high / len(cuts)))
        gain = gain * jnp.repeat(steps, extent[position] // parts).reshape([-1 if axis == position else 1 for axis in range(len(extent))])
    return gain


def scatter_about(rng, shape, width, most, cuts=(), held_as=jnp.bfloat16):
    entries = jax.random.normal(rng, shape, jnp.float32) * width
    if len(cuts) > 0:
        entries = levels(rng, shape, cuts, -0.22, 0.18) * entries
    return jnp.clip(entries, min=-most, max=most).astype(held_as)


def setup_inputs(seed: int = 0) -> dict:
    seeds = jax.random.split(jax.random.key(seed), 7)
    fields = scatter_about(seeds[0], (2, PORTS, 6, NX, NY, NZ), 1.0, 6.0, ((1, 8), (3, 32)), jnp.float32)
    inv_eps = jnp.clip(jnp.exp(math.log(0.48) - 2.4849066 * jax.random.uniform(seeds[1], (3, NX, NY, NZ), jnp.float32) ** levels(seeds[1], (3, NX, NY, NZ), ((1, 32),), -0.2, 0.2)), 0.04, 0.48)
    tensor_tiles = draw_tensor_tiles(jax.random.fold_in(seeds[6], 71), 0)
    tile_index = draw_tile_index(jax.random.fold_in(seeds[6], 71), 0)
    ports = plant(jax.random.randint(seeds[4], (2, PORTS), 0, NX * NY * NZ), jax.random.fold_in(seeds[4], 1), 0, (NX * NY * NZ) - 1).astype(jnp.int32)
    waves = scatter_about(seeds[5], (2, PORTS, STEPS), 2.0, 8.0, ((1, 8),), jnp.float32)
    return {"fields": fields, "inv_eps": inv_eps, "tensor_tiles": tensor_tiles, "tile_index": tile_index, "ports": ports, "waves": waves}


magnetic_coef = 0.5

def forward_cell(values, along):
    widths = [(0, 0)] * values.ndim
    widths[along] = (0, 1)
    return lax.slice_in_dim(jnp.pad(values, widths), 1, values.shape[along] + 1, axis=along)

def backward_cell(values, along):
    widths = [(0, 0)] * values.ndim
    widths[along] = (1, 0)
    return lax.slice_in_dim(jnp.pad(values, widths), 0, values.shape[along], axis=along)

def magnetic_update(magnetic, electric, elec_y_up, elec_z_up):
    elec_x, elec_y, elec_z = (electric[:, 0], electric[:, 1], electric[:, 2])
    magn_x = magnetic[:, 0] - magnetic_coef * (forward_cell(elec_z, 2) - elec_z - (forward_cell(elec_y, 3) - elec_y))
    magn_y = magnetic[:, 1] - magnetic_coef * (forward_cell(elec_x, 3) - elec_x - (elec_z_up - elec_z))
    magn_z = magnetic[:, 2] - magnetic_coef * (elec_y_up - elec_y - (forward_cell(elec_x, 2) - elec_x))
    return jnp.stack([magn_x, magn_y, magn_z], 1)

def electric_update(electric, magnetic, magn_y_down, magn_z_down, tensor):
    magn_x, magn_y, magn_z = (magnetic[:, 0], magnetic[:, 1], magnetic[:, 2])
    curl_x = magn_z - backward_cell(magn_z, 2) - (magn_y - backward_cell(magn_y, 3))
    curl_y = magn_x - backward_cell(magn_x, 3) - (magn_z - magn_z_down)
    curl_z = magn_y - magn_y_down - (magn_x - backward_cell(magn_x, 2))
    elec_x = electric[:, 0] + (tensor[0] * curl_x + tensor[3] * curl_y + tensor[4] * curl_z)
    elec_y = electric[:, 1] + (tensor[3] * curl_x + tensor[1] * curl_y + tensor[5] * curl_z)
    elec_z = electric[:, 2] + (tensor[4] * curl_x + tensor[5] * curl_y + tensor[2] * curl_z)
    return (elec_x, elec_y, elec_z)

def build_tensor(inv_eps, tensor_tiles, tile_index):
    bulk = jnp.concatenate([inv_eps, jnp.zeros_like(inv_eps)], 0).reshape(6, NX * NY, NZ)
    tiles = tensor_tiles.reshape(SLABS, SLABS, CAP, 6, NZ).transpose(1, 0, 2, 3, 4)
    owner = jnp.arange(SLABS).astype(jnp.int32).reshape(SLABS, 1, 1)
    columns = jnp.where(tile_index >= 0, owner * (CX * NY) + tile_index, NX * NY).astype(jnp.int32)
    rows_in = tiles.reshape(SLABS * SLABS * CAP, 6, NZ).transpose(1, 0, 2)
    bulk = bulk.at[:, columns.reshape(-1)].set(rows_in, mode='drop')
    return bulk.reshape(6, NX, NY, NZ)

def reference(fields, inv_eps, tensor_tiles, tile_index, ports, waves):
    tensor = build_tensor(inv_eps, tensor_tiles, tile_index)
    plane = NY * NZ

    def one_port(inputs):
        start, source_cells, pulses = inputs
        electric = start[:, :3]
        magnetic = start[:, 3:]
        cell_x = (source_cells // plane).astype(jnp.int32)
        cell_y = (source_cells % plane // NZ).astype(jnp.int32)
        cell_z = (source_cells % NZ).astype(jnp.int32)
        sim_ids = jnp.arange(2).astype(jnp.int32)
        summed = jnp.zeros((NX, NY, NZ), jnp.float32)
        for time_step in range(STEPS):
            magnetic = magnetic_update(magnetic, electric, forward_cell(electric[:, 1], 1), forward_cell(electric[:, 2], 1))
            elec_x, elec_y, elec_z = electric_update(electric, magnetic, backward_cell(magnetic[:, 1], 1), backward_cell(magnetic[:, 2], 1), tensor)
            elec_z = elec_z.at[sim_ids, cell_x, cell_y, cell_z].add(pulses[:, time_step])
            summed = summed + (elec_x[0] * elec_x[1] + elec_y[0] * elec_y[1] + elec_z[0] * elec_z[1])
            electric = jnp.stack([elec_x, elec_y, elec_z], 1)
        return (jnp.concatenate([electric, magnetic], 1), summed)
    finals, summed_all = lax.map(one_port, (fields.transpose(1, 0, 2, 3, 4, 5), ports.T, waves.transpose(1, 0, 2)))
    fields_out = finals.transpose(1, 0, 2, 3, 4, 5)
    correlation = lax.optimization_barrier(jnp.sum(summed_all, axis=0))
    sensitivity = correlation * (1.0 / math.sqrt(PORTS * STEPS))
    return (fields_out, sensitivity)
```

```python
import functools
import math

import jax
import jax.numpy as jnp
from jax import lax
from jax.experimental import pallas as pl
from jax.experimental.pallas import tpu as pltpu
from jax.sharding import PartitionSpec as P

magnetic_coef = 0.5
chunk = 8
in_vmem = pl.BlockSpec(memory_space=pltpu.VMEM)
in_smem = pl.BlockSpec(memory_space=pltpu.SMEM)
in_any = pl.BlockSpec(memory_space=pl.ANY)
params = pltpu.CompilerParams(vmem_limit_bytes=48 * 1024 * 1024)


def next_z(values, lane):
    size = values.shape[1]
    return jnp.where(lane < size - 1, pltpu.roll(values, size - 1, 1), 0.0)


def prev_z(values, lane):
    return jnp.where(lane > 0, pltpu.roll(values, 1, 1), 0.0)


def lanes(elec):
    return lax.broadcasted_iota(jnp.int32, (chunk, elec.shape[-1]), 1)


def each_chunk(rows, body):
    def step(c, carry):
        body(pl.multiple_of(c * chunk, chunk))
        return carry

    lax.fori_loop(0, rows // chunk, step, 0)


def magnetic_planes(elec, magn, planes, y0, lane, low_coef):
    new = {}
    old = {}

    def load(sim, comp, x):
        if (sim, comp, x) not in old:
            old[sim, comp, x] = elec[sim, comp, x, pl.ds(y0, chunk), :]
        return old[sim, comp, x]

    for sim in range(2):
        for x in planes:
            coef = low_coef if x == 0 else magnetic_coef
            elec_x, elec_y, elec_z = (load(sim, comp, x) for comp in range(3))
            x_up_y = elec[sim, 0, x, pl.ds(y0 + 1, chunk), :]
            z_up_y = elec[sim, 2, x, pl.ds(y0 + 1, chunk), :]
            y_up_x = load(sim, 1, x + 1)
            z_up_x = load(sim, 2, x + 1)
            curls = (
                z_up_y - elec_z - (next_z(elec_y, lane) - elec_y),
                next_z(elec_x, lane) - elec_x - (z_up_x - elec_z),
                y_up_x - elec_y - (x_up_y - elec_x),
            )
            for comp, curl in enumerate(curls):
                spot = (sim, comp, x, pl.ds(y0 + chunk, chunk), slice(None))
                new[sim, comp, x] = magn[spot] - coef * curl
                magn[spot] = new[sim, comp, x]
    return new, load


def add_products(corr, load, width_x, y0):
    for x in range(width_x):
        terms = [load(0, comp, x + 1) * load(1, comp, x + 1) for comp in range(3)]
        corr[x, pl.ds(y0, chunk), :] += terms[0] + terms[1] + terms[2]


def electric_planes(elec, magn, tensor_at, below_at, planes, y0, lane, top):
    cur = pl.ds(y0 + chunk, chunk)
    prev = pl.ds(y0 + chunk - 1, chunk)
    for x in planes:
        tensor = tensor_at(x)
        for sim in range(2):
            magn_x, magn_y, magn_z = (magn[sim, comp, x, cur, :] for comp in range(3))
            x_down_y = magn[sim, 0, x, prev, :]
            z_down_y = magn[sim, 2, x, prev, :]
            y_down_x, z_down_x = below_at(sim) if x == 0 else (magn[sim, 1, x - 1, cur, :], magn[sim, 2, x - 1, cur, :])
            curl_x = magn_z - z_down_y - (magn_y - prev_z(magn_y, lane))
            curl_y = magn_x - prev_z(magn_x, lane) - (magn_z - z_down_x)
            curl_z = magn_y - y_down_x - (magn_x - x_down_y)
            rows = ((0, 3, 4), (3, 1, 5), (4, 5, 2))
            for comp in range(3):
                if x == top and comp == 0:
                    continue
                a, b, c = (tensor[i] for i in rows[comp])
                spot = (sim, comp, x, pl.ds(y0, chunk), slice(None))
                elec[spot] = elec[spot] + (a * curl_x + b * curl_y + c * curl_z)


def add_sources(elec, info, ports, waves, time_step, first, last):
    rows, size = elec.shape[3] - chunk, elec.shape[4]
    plane = rows * size
    width_x = elec.shape[2] - 2
    lane = lax.broadcasted_iota(jnp.int32, (1, size), 1)
    for sim in range(2):
        cell = ports[sim, info[1]]
        x = cell // plane - info[0] * width_x + 1
        rest = cell % plane

        @pl.when((x >= first) & (x <= last))
        def _():
            spot = (sim, 2, x, pl.ds(rest // size, 1), slice(None))
            elec[spot] = elec[spot] + jnp.where(lane == rest % size, waves[sim, 0, time_step], 0.0)


def write_messages(new, load, even, y0, width_x, to_core, to_chip, extra_at):
    top = width_x
    up_parts, down_parts = [], []
    for sim in range(2):
        up_parts += [new[sim, 1, top - 1], new[sim, 2, top - 1]]
        up_parts += [load(sim, comp, top) for comp in range(3)]
        down_parts += [new[sim, comp, 1] for comp in range(3)]
        down_parts += [load(sim, comp, 1) for comp in (1, 2)]
    if extra_at is not None:
        for sim in range(2):
            for comp in range(3):
                up_parts.append(extra_at(sim, comp))
                down_parts.append(new[sim, comp, 1])
    for i, (up, down) in enumerate(zip(up_parts, down_parts)):
        to_core[i, pl.ds(y0, chunk), :] = jnp.where(even, up, down)
        to_chip[i, pl.ds(y0, chunk), :] = jnp.where(even, down, up)


def start_kernel(info, fields, elec, magn, to_core, to_chip, sems):
    width_x = elec.shape[2] - 2
    rows = elec.shape[3] - chunk
    copies = []
    for sim in range(2):
        copies.append(
            pltpu.make_async_copy(
                fields.at[sim, 0, pl.ds(0, 3)],
                elec.at[sim, :, pl.ds(1, width_x), pl.ds(0, rows)],
                sems.at[sim, 0],
            )
        )
        copies.append(
            pltpu.make_async_copy(
                fields.at[sim, 0, pl.ds(3, 3)],
                magn.at[sim, :, pl.ds(1, width_x), pl.ds(chunk, rows)],
                sems.at[sim, 1],
            )
        )
    for copy in copies:
        copy.start()
    zeros = jnp.zeros((chunk, elec.shape[4]), jnp.float32)
    for sim in range(2):
        for comp in range(3):
            for x in range(width_x + 2):
                elec[sim, comp, x, pl.ds(rows, chunk), :] = zeros
                magn[sim, comp, x, pl.ds(0, chunk), :] = zeros
    for copy in copies:
        copy.wait()
    even = info[2] == 0
    lane = lanes(elec)

    def prepare(y0):
        new, load = magnetic_planes(elec, magn, range(1, width_x), y0, lane, None)

        def extra_at(sim, comp):
            return magn[sim, comp, width_x, pl.ds(y0 + chunk, chunk), :]

        write_messages(new, load, even, y0, width_x, to_core, to_chip, extra_at)

    each_chunk(rows, prepare)


def tensor_kernel(info, index, inv_eps, tiles, tensor, to_core, to_chip):
    width_x, rows, size = inv_eps.shape[1:]
    slabs, slots = index.shape[1:]
    columns = width_x * rows
    zeros = jnp.zeros((chunk, size), jnp.float32)

    def fill(c, carry):
        y0 = pl.multiple_of(c * chunk, chunk)
        for comp in range(3):
            for x in range(width_x):
                spot = pl.ds(pl.multiple_of(x * rows + y0, chunk), chunk)
                tensor[comp, spot, :] = inv_eps[comp, x, pl.ds(y0, chunk), :]
                tensor[comp + 3, spot, :] = zeros
        return carry

    lax.fori_loop(0, rows // chunk, fill, 0)

    def place(owner, carry):
        for k in range(slots):
            column = index[0, owner, k]
            column = jnp.where(column < 0, columns, column)
            for entry in range(6):
                tensor[entry, pl.ds(column, 1), :] = tiles[owner, pl.ds(6 * k + entry, 1), :]
        return carry

    lax.fori_loop(0, slabs, place, 0)
    even = info[2] == 0
    for entry in range(6):
        first = tensor[entry, pl.ds(0, rows), :]
        last = tensor[entry, pl.ds((width_x - 1) * rows, rows), :]
        to_core[entry] = jnp.where(even, last, first)
        to_chip[entry] = jnp.where(even, first, last)


def pair_kernel(time_step, opening, closing, *refs):
    info, ports, waves, elec_in, magn_in, tensor, corr_in, tensor_core, tensor_chip, from_core, from_chip = refs[:11]
    if closing:
        fields_out, elec, magn, corr, sems = refs[11:]
    else:
        elec, magn, corr, to_core, to_chip = refs[11:]
    width_x = elec.shape[2] - 2
    rows = elec.shape[3] - chunk
    top = width_x + 1
    even = info[2] == 0
    low_coef = jnp.where(info[0] == 0, 0.0, magnetic_coef)
    lane = lanes(elec)

    def below(i, y0):
        spot = (i, pl.ds(y0, chunk), slice(None))
        return jnp.where(even, from_chip[spot], from_core[spot])

    def above(i, y0):
        spot = (i, pl.ds(y0, chunk), slice(None))
        return jnp.where(even, from_core[spot], from_chip[spot])

    def unpack(y0):
        for sim in range(2):
            for comp in range(3):
                elec[sim, comp, 0, pl.ds(y0, chunk), :] = below(5 * sim + 2 + comp, y0)
                magn[sim, comp, top, pl.ds(y0 + chunk, chunk), :] = above(5 * sim + comp, y0)
                if opening:
                    magn[sim, comp, 0, pl.ds(y0 + chunk, chunk), :] = below(10 + 3 * sim + comp, y0)
            for comp in (1, 2):
                elec[sim, comp, top, pl.ds(y0, chunk), :] = above(5 * sim + 2 + comp, y0)
        if opening:
            for x in range(width_x):
                corr[x, pl.ds(y0, chunk), :] = jnp.zeros((chunk, elec.shape[4]), jnp.float32)

    each_chunk(rows, unpack)

    if opening:
        @pl.when(info[0] == 0)
        def _():
            for sim in range(2):
                for comp in range(3):
                    magn[sim, comp, 0] = jnp.zeros(magn.shape[3:], jnp.float32)

    def tensor_of(y0):
        def at(x):
            if 0 < x < top:
                spot = pl.ds(pl.multiple_of((x - 1) * rows + y0, chunk), chunk)
                return [tensor[i, spot, :] for i in range(6)]
            spot = pl.ds(y0, chunk)
            low = even if x == 0 else jnp.logical_not(even)
            return [jnp.where(low, tensor_chip[i, spot, :], tensor_core[i, spot, :]) for i in range(6)]

        return at

    def below_of(y0):
        return lambda sim: (below(5 * sim, y0), below(5 * sim + 1, y0))

    def magnetic_edges(y0):
        magnetic_planes(elec, magn, (0, width_x), y0, lane, low_coef)

    def electric_wide(y0):
        electric_planes(elec, magn, tensor_of(y0), below_of(y0), range(top + 1), y0, lane, top)

    def magnetic_all(y0):
        _, load = magnetic_planes(elec, magn, range(top), y0, lane, low_coef)
        add_products(corr, load, width_x, y0)

    def electric_own(y0):
        electric_planes(elec, magn, tensor_of(y0), None, range(1, top), y0, lane, top)

    each_chunk(rows, magnetic_edges)
    each_chunk(rows, electric_wide)
    add_sources(elec, info, ports, waves, time_step, 0, top)
    each_chunk(rows, magnetic_all)
    copies = []
    if closing:
        for sim in range(2):
            copies.append(
                pltpu.make_async_copy(
                    magn.at[sim, :, pl.ds(1, width_x), pl.ds(chunk, rows)],
                    fields_out.at[sim, 0, pl.ds(3, 3)],
                    sems.at[sim, 1],
                )
            )
            copies[-1].start()
    each_chunk(rows, electric_own)
    add_sources(elec, info, ports, waves, time_step + 1, 1, width_x)
    if closing:
        for sim in range(2):
            copies.append(
                pltpu.make_async_copy(
                    elec.at[sim, :, pl.ds(1, width_x), pl.ds(0, rows)],
                    fields_out.at[sim, 0, pl.ds(0, 3)],
                    sems.at[sim, 0],
                )
            )
            copies[-1].start()

        def finish(y0):
            def load(sim, comp, x):
                return elec[sim, comp, x, pl.ds(y0, chunk), :]

            add_products(corr, load, width_x, y0)

        each_chunk(rows, finish)
        for copy in copies:
            copy.wait()
    else:

        def prepare(y0):
            new, load = magnetic_planes(elec, magn, range(1, width_x), y0, lane, None)
            add_products(corr, load, width_x, y0)
            write_messages(new, load, even, y0, width_x, to_core, to_chip, None)

        each_chunk(rows, prepare)


def local(fields, inv_eps, tensor_tiles, tile_index, ports, waves):
    slab_rank = lax.axis_index("space")
    port_rank = lax.axis_index("port")
    slabs = lax.axis_size("space")
    width_x, rows, size = fields.shape[3:]
    steps_total = waves.shape[2]
    port_total = ports.shape[1]
    info = jnp.stack([slab_rank, port_rank, slab_rank % 2]).astype(jnp.int32)
    core_pairs = [(i, i ^ 1) for i in range(slabs)]
    chip_pairs = [(i, ((i + 1) ^ 1) - 1) for i in range(1, slabs - 1)]

    def exchange(to_core, to_chip):
        return lax.ppermute(to_core, "space", core_pairs), lax.ppermute(to_chip, "space", chip_pairs)

    def held(*shape):
        return pltpu.VMEM(shape, jnp.float32)

    elec_shape = held(2, 3, width_x + 2, rows + chunk, size)
    corr_shape = held(width_x, rows, size)
    wire = lambda n: jax.ShapeDtypeStruct((n, rows, size), jnp.float32)

    elec, magn, to_core, to_chip = pl.pallas_call(
        start_kernel,
        name="start",
        out_shape=(elec_shape, elec_shape, wire(16), wire(16)),
        in_specs=[in_smem, in_any],
        out_specs=[in_vmem] * 4,
        scratch_shapes=[pltpu.SemaphoreType.DMA((2, 2))],
        compiler_params=params,
    )(info, fields)
    from_core, from_chip = exchange(to_core, to_chip)
    arrived = lax.all_to_all(tensor_tiles, "space", split_axis=1, concat_axis=0, tiled=True)
    arrived = arrived.reshape(arrived.shape[0], *arrived.shape[2:])
    tensor, face_core, face_chip = pl.pallas_call(
        tensor_kernel,
        name="tensor",
        out_shape=(held(6, width_x * rows + chunk, size), wire(6), wire(6)),
        in_specs=[in_smem, in_smem, in_vmem, in_vmem],
        out_specs=[in_vmem] * 3,
        compiler_params=params,
    )(info, tile_index, inv_eps, arrived)
    tensor_core, tensor_chip = exchange(face_core, face_chip)
    corr = None
    for time_step in range(0, steps_total, 2):
        opening = time_step == 0
        closing = time_step + 2 >= steps_total
        if opening:
            corr = jnp.zeros((width_x, rows, size), jnp.float32)
        state = (elec_shape, elec_shape, corr_shape)
        wires = (wire(10), wire(10))
        whole = jax.ShapeDtypeStruct(fields.shape, jnp.float32)
        base = 1 if closing else 0
        outs = pl.pallas_call(
            functools.partial(pair_kernel, time_step, opening, closing),
            name="pair",
            out_shape=(whole, *state) if closing else (*state, *wires),
            in_specs=[in_smem] * 3 + [in_vmem] * 8,
            out_specs=[in_any] + [in_vmem] * 3 if closing else [in_vmem] * 5,
            scratch_shapes=[pltpu.SemaphoreType.DMA((2, 2))] if closing else [],
            input_output_aliases={3: base, 4: base + 1, 6: base + 2},
            compiler_params=params,
        )(info, ports, waves, elec, magn, tensor, corr, tensor_core, tensor_chip, from_core, from_chip)
        if closing:
            fields_out, _, _, corr = outs
        else:
            elec, magn, corr, to_core, to_chip = outs
            from_core, from_chip = exchange(to_core, to_chip)
    shares = lax.all_to_all(corr, "port", split_axis=1, concat_axis=0, tiled=True)
    reduced = jnp.sum(shares.reshape(-1, width_x, *shares.shape[1:]), axis=0)
    sensitivity = reduced * (1.0 / math.sqrt(port_total * steps_total))
    return (fields_out, sensitivity)


def solution(mesh):
    in_specs = (
        P(None, "port", None, "space", None, None),
        P(None, "space", None, None),
        P("space", None, None, None),
        P("space", None, None),
        P(),
        P(None, "port", None),
    )
    out_specs = (P(None, "port", None, "space", None, None), P("space", "port", None))
    return jax.shard_map(local, mesh=mesh, in_specs=in_specs, out_specs=out_specs, check_vma=False)
```

```python
import functools
import math

import jax
import jax.numpy as jnp
from jax import lax
from jax.experimental import pallas as pl
from jax.experimental.pallas import tpu as pltpu
from jax.sharding import PartitionSpec as P

magnetic_coef = 0.5
chunk = 8
unroll = 4
in_vmem = pl.BlockSpec(memory_space=pltpu.VMEM)
in_smem = pl.BlockSpec(memory_space=pltpu.SMEM)
in_any = pl.BlockSpec(memory_space=pl.ANY)
params = pltpu.CompilerParams(vmem_limit_bytes=48 * 1024 * 1024)


def next_z(values, lane):
    size = values.shape[1]
    return jnp.where(lane < size - 1, pltpu.roll(values, size - 1, 1), 0.0)


def prev_z(values, lane):
    return jnp.where(lane > 0, pltpu.roll(values, 1, 1), 0.0)


class Slab:
    def __init__(self, elec, magn, tensor=None, corr=None):
        self.elec, self.magn, self.tensor, self.corr = elec, magn, tensor, corr
        self.width_x = elec.shape[2] - 2
        self.rows = elec.shape[3] - chunk
        self.lane = lax.broadcasted_iota(jnp.int32, (chunk, elec.shape[4]), 1)

    def e(self, sim, comp, cell, y0):
        return self.elec[sim, comp, cell + 1, pl.ds(y0, chunk), :]

    def h(self, sim, comp, cell, y0):
        return self.magn[sim, comp, cell + 2, pl.ds(y0 + chunk, chunk), :]

    def put_e(self, sim, comp, cell, y0, values):
        self.elec[sim, comp, cell + 1, pl.ds(y0, chunk), :] = values

    def put_h(self, sim, comp, cell, y0, values):
        self.magn[sim, comp, cell + 2, pl.ds(y0 + chunk, chunk), :] = values

    def tensor_at(self, cell, y0):
        spot = pl.ds(pl.multiple_of((cell + 1) * self.rows + y0, chunk), chunk)
        return [self.tensor[i, spot, :] for i in range(6)]

    def put_tensor(self, cell, y0, entry, values):
        spot = pl.ds(pl.multiple_of((cell + 1) * self.rows + y0, chunk), chunk)
        self.tensor[entry, spot, :] = values

    def each_chunk(self, *bodies):
        for body in bodies:

            def step(c, carry):
                for u in range(unroll):
                    body(pl.multiple_of((c * unroll + u) * chunk, chunk))
                return carry

            lax.fori_loop(0, self.rows // (chunk * unroll), step, 0)

    def magnetic(self, cells, low_coef=magnetic_coef):
        def body(y0):
            for sim in range(2):
                for cell in cells:
                    coef = low_coef if cell == -1 else magnetic_coef
                    elec_x, elec_y, elec_z = (self.e(sim, comp, cell, y0) for comp in range(3))
                    x_up_y, z_up_y = self.e(sim, 0, cell, y0 + 1), self.e(sim, 2, cell, y0 + 1)
                    y_up_x, z_up_x = self.e(sim, 1, cell + 1, y0), self.e(sim, 2, cell + 1, y0)
                    curls = (
                        z_up_y - elec_z - (next_z(elec_y, self.lane) - elec_y),
                        next_z(elec_x, self.lane) - elec_x - (z_up_x - elec_z),
                        y_up_x - elec_y - (x_up_y - elec_x),
                    )
                    for comp, curl in enumerate(curls):
                        self.put_h(sim, comp, cell, y0, self.h(sim, comp, cell, y0) - coef * curl)

        self.each_chunk(body)

    def electric(self, cells):
        def body(y0):
            for cell in cells:
                txx, tyy, tzz, txy, txz, tyz = self.tensor_at(cell, y0)
                for sim in range(2):
                    magn_x, magn_y, magn_z = (self.h(sim, comp, cell, y0) for comp in range(3))
                    x_down_y, z_down_y = self.h(sim, 0, cell, y0 - 1), self.h(sim, 2, cell, y0 - 1)
                    y_down_x, z_down_x = self.h(sim, 1, cell - 1, y0), self.h(sim, 2, cell - 1, y0)
                    curl_x = magn_z - z_down_y - (magn_y - prev_z(magn_y, self.lane))
                    curl_y = magn_x - prev_z(magn_x, self.lane) - (magn_z - z_down_x)
                    curl_z = magn_y - y_down_x - (magn_x - x_down_y)
                    rows = ((txx, txy, txz), (txy, tyy, tyz), (txz, tyz, tzz))
                    for comp in range(1 if cell == self.width_x else 0, 3):
                        a, b, c = rows[comp]
                        change = a * curl_x + b * curl_y + c * curl_z
                        self.put_e(sim, comp, cell, y0, self.e(sim, comp, cell, y0) + change)

        self.each_chunk(body)

    def correlate(self, cells):
        def body(y0):
            for cell in cells:
                terms = [self.e(0, comp, cell, y0) * self.e(1, comp, cell, y0) for comp in range(3)]
                self.corr[y0 // chunk, cell] += terms[0] + terms[1] + terms[2]

        self.each_chunk(body)

    def sources(self, info, ports, waves, time_step, cells):
        size = self.elec.shape[4]
        plane = self.rows * size
        lane = lax.broadcasted_iota(jnp.int32, (1, size), 1)
        for sim in range(2):
            source = ports[sim, info[1]]
            cell = source // plane - info[0] * self.width_x
            rest = source % plane

            @pl.when((cell >= cells[0]) & (cell <= cells[-1]))
            def _():
                spot = (sim, 2, cell + 1, pl.ds(rest // size, 1), slice(None))
                self.elec[spot] = self.elec[spot] + jnp.where(lane == rest % size, waves[sim, 0, time_step], 0.0)

    def send_up(self, message):
        def body(y0):
            top = self.width_x - 1
            for sim in range(2):
                parts = [self.h(sim, comp, top - 1, y0) for comp in (1, 2)]
                parts += [self.e(sim, comp, top, y0) for comp in range(3)]
                for i, part in enumerate(parts):
                    message[5 * sim + i, pl.ds(y0, chunk), :] = part
                if message.shape[0] > 10:
                    for comp in range(3):
                        message[10 + 3 * sim + comp, pl.ds(y0, chunk), :] = self.h(sim, comp, top, y0)

        self.each_chunk(body)

    def send_down(self, message):
        def body(y0):
            for sim in range(2):
                parts = [self.h(sim, comp, 0, y0) for comp in range(3)] + [self.e(sim, comp, 0, y0) for comp in (1, 2)]
                for i, part in enumerate(parts):
                    message[5 * sim + i, pl.ds(y0, chunk), :] = part
                if message.shape[0] > 10:
                    for comp in range(3):
                        message[10 + 3 * sim + comp, pl.ds(y0, chunk), :] = parts[comp]

        self.each_chunk(body)

    def take_below(self, message, faces):
        def body(y0):
            spot = pl.ds(y0, chunk)
            for sim in range(2):
                for comp in (1, 2):
                    self.put_h(sim, comp, -2, y0, message[5 * sim + comp - 1, spot, :])
                for comp in range(3):
                    self.put_e(sim, comp, -1, y0, message[5 * sim + 2 + comp, spot, :])
                    if faces is not None:
                        self.put_h(sim, comp, -1, y0, message[10 + 3 * sim + comp, spot, :])
            if faces is not None:
                for entry in range(6):
                    self.put_tensor(-1, y0, entry, faces[entry, spot, :])

        self.each_chunk(body)

    def take_above(self, message, faces):
        def body(y0):
            spot = pl.ds(y0, chunk)
            for sim in range(2):
                for comp in range(3):
                    self.put_h(sim, comp, self.width_x, y0, message[5 * sim + comp, spot, :])
                for comp in (1, 2):
                    self.put_e(sim, comp, self.width_x, y0, message[5 * sim + 2 + comp, spot, :])
            if faces is not None:
                for entry in range(6):
                    self.put_tensor(self.width_x, y0, entry, faces[entry, spot, :])

        self.each_chunk(body)

    def copies_out(self, fields_out, first, count, sems):
        return [
            pltpu.make_async_copy(
                self.elec.at[sim, :, pl.ds(first + 1, count), pl.ds(0, self.rows)],
                fields_out.at[sim, 0, pl.ds(0, 3), pl.ds(first, count)],
                sems.at[sim, 0],
            )
            for sim in range(2)
        ], [
            pltpu.make_async_copy(
                self.magn.at[sim, :, pl.ds(first + 2, count), pl.ds(chunk, self.rows)],
                fields_out.at[sim, 0, pl.ds(3, 3), pl.ds(first, count)],
                sems.at[sim, 1],
            )
            for sim in range(2)
        ]


def start_kernel(info, fields, elec, magn, corr, to_core, to_chip, sems):
    slab = Slab(elec, magn)
    width_x, rows = slab.width_x, slab.rows
    copies = []
    for sim in range(2):
        copies.append(
            pltpu.make_async_copy(
                fields.at[sim, 0, pl.ds(0, 3)],
                elec.at[sim, :, pl.ds(1, width_x), pl.ds(0, rows)],
                sems.at[sim, 0],
            )
        )
        copies.append(
            pltpu.make_async_copy(
                fields.at[sim, 0, pl.ds(3, 3)],
                magn.at[sim, :, pl.ds(2, width_x), pl.ds(chunk, rows)],
                sems.at[sim, 1],
            )
        )
    for copy in copies:
        copy.start()
    zeros = jnp.zeros((chunk, elec.shape[4]), jnp.float32)
    for sim in range(2):
        for comp in range(3):
            for x in range(elec.shape[2]):
                elec[sim, comp, x, pl.ds(rows, chunk), :] = zeros
            for x in range(magn.shape[2]):
                magn[sim, comp, x, pl.ds(0, chunk), :] = zeros
    corr[...] = jnp.zeros(corr.shape, jnp.float32)
    for copy in copies:
        copy.wait()
    slab.magnetic((0, width_x - 2))

    @pl.when(info[2] == 0)
    def _():
        slab.send_down(to_chip)
        slab.send_up(to_core)

    @pl.when(info[2] == 1)
    def _():
        slab.send_up(to_chip)
        slab.send_down(to_core)


def tensor_kernel(info, index, inv_eps, tiles, tensor, to_core, to_chip):
    width_x, rows, size = inv_eps.shape[1:]
    slabs, slots = index.shape[1:]
    spare = (width_x + 2) * rows
    zeros = jnp.zeros((chunk, size), jnp.float32)

    def fill(c, carry):
        y0 = pl.multiple_of(c * chunk, chunk)
        for comp in range(3):
            for x in range(width_x):
                spot = pl.ds(pl.multiple_of((x + 1) * rows + y0, chunk), chunk)
                tensor[comp, spot, :] = inv_eps[comp, x, pl.ds(y0, chunk), :]
                tensor[comp + 3, spot, :] = zeros
        return carry

    lax.fori_loop(0, rows // chunk, fill, 0)

    def place(owner, carry):
        for k in range(slots):
            column = index[0, owner, k]
            column = jnp.where(column < 0, spare, column + rows)
            for entry in range(6):
                tensor[entry, pl.ds(column, 1), :] = tiles[owner, pl.ds(6 * k + entry, 1), :]
        return carry

    lax.fori_loop(0, slabs, place, 0)
    even = info[2] == 0
    for entry in range(6):
        first = tensor[entry, pl.ds(rows, rows), :]
        last = tensor[entry, pl.ds(width_x * rows, rows), :]
        to_core[entry] = jnp.where(even, last, first)
        to_chip[entry] = jnp.where(even, first, last)


def far_kernel(time_step, opening, closing, *refs):
    info, ports, waves, _, _, tensor, _, from_core = refs[:8]
    faces = refs[8] if opening else None
    refs = refs[9:] if opening else refs[8:]
    if closing:
        elec, magn, corr, fields_out, sems = refs
    elif opening:
        elec, magn, corr, tensor, to_core = refs
    else:
        elec, magn, corr, to_core = refs
    slab = Slab(elec, magn, tensor, corr)
    top = slab.width_x

    def advance(edge, wide, own, middle, last, next_edge):
        slab.magnetic((edge, 1))
        slab.electric(wide)
        slab.sources(info, ports, waves, time_step, wide)
        slab.correlate(own)
        slab.magnetic(middle)
        slab.electric(last)
        slab.sources(info, ports, waves, time_step + 1, last)
        slab.correlate(last)
        if not closing:
            slab.magnetic((next_edge,))

    @pl.when(info[2] == 0)
    def _():
        slab.take_above(from_core, faces)
        advance(top - 1, range(1, top + 1), range(1, top), range(1, top), range(2, top), top - 2)
        if not closing:
            slab.send_up(to_core)

    @pl.when(info[2] == 1)
    def _():
        slab.take_below(from_core, faces)
        advance(-1, range(-1, top - 1), range(top - 1), range(-1, top - 2), range(top - 2), 0)
        if not closing:
            slab.send_down(to_core)

    if closing:
        first = jnp.where(info[2] == 0, 2, 0)
        elec_copies, magn_copies = slab.copies_out(fields_out, first, 2, sems)
        for copy in elec_copies + magn_copies:
            copy.start()
        for copy in elec_copies + magn_copies:
            copy.wait()


def near_kernel(time_step, opening, closing, *refs):
    info, ports, waves, _, _, tensor, _, from_chip = refs[:8]
    faces = refs[8] if opening else None
    refs = refs[9:] if opening or closing else refs[8:]
    if closing:
        elec, magn, corr, fields_out, sems = refs
    elif opening:
        elec, magn, corr, tensor, to_chip = refs
    else:
        elec, magn, corr, to_chip = refs
    slab = Slab(elec, magn, tensor, corr)
    top = slab.width_x
    low_coef = jnp.where(info[0] == 0, 0.0, magnetic_coef)
    copies = []
    first = jnp.where(info[2] == 0, 0, 2)

    def advance(edge, wide, own, middle, last, next_edge):
        slab.magnetic((edge,), low_coef)
        slab.electric(wide)
        slab.sources(info, ports, waves, time_step, wide)
        slab.correlate(own)
        slab.magnetic(middle, low_coef)
        slab.electric(last)
        slab.sources(info, ports, waves, time_step + 1, last)
        slab.correlate(last)
        if not closing:
            slab.magnetic((next_edge,))

    @pl.when(info[2] == 0)
    def _():
        slab.take_below(from_chip, faces)
        advance(-1, (-1, 0), (0,), (-1, 0), (0, 1), 0)
        if not closing:
            slab.send_down(to_chip)

    @pl.when(info[2] == 1)
    def _():
        slab.take_above(from_chip, faces)
        advance(top - 1, (top - 1, top), (top - 1,), (top - 2, top - 1), (top - 2, top - 1), top - 2)
        if not closing:
            slab.send_up(to_chip)

    if closing:
        elec_copies, magn_copies = slab.copies_out(fields_out, first, 2, sems)
        for copy in elec_copies + magn_copies:
            copy.start()
        for copy in elec_copies + magn_copies:
            copy.wait()


def sum_kernel(scale, shares, total):
    acc = shares[0]
    for i in range(1, shares.shape[0]):
        acc = acc + shares[i]
    total[...] = acc * scale


def local(fields, inv_eps, tensor_tiles, tile_index, ports, waves):
    slab_rank = lax.axis_index("space")
    port_rank = lax.axis_index("port")
    slabs = lax.axis_size("space")
    width_x, rows, size = fields.shape[3:]
    steps_total = waves.shape[2]
    port_total = ports.shape[1]
    info = jnp.stack([slab_rank, port_rank, slab_rank % 2]).astype(jnp.int32)
    core_pairs = [(i, i ^ 1) for i in range(slabs)]
    chip_pairs = [(i, ((i + 1) ^ 1) - 1) for i in range(1, slabs - 1)]

    def by_core(message):
        return lax.ppermute(message, "space", core_pairs)

    def by_chip(message):
        return lax.ppermute(message, "space", chip_pairs)

    def held(*shape):
        return pltpu.VMEM(shape, jnp.float32)

    elec_shape = held(2, 3, width_x + 2, rows + chunk, size)
    magn_shape = held(2, 3, width_x + 3, rows + chunk, size)
    corr_shape = held(rows // chunk, width_x, chunk, size)
    tensor_shape = held(6, (width_x + 2) * rows + chunk, size)
    whole = jax.ShapeDtypeStruct(fields.shape, jnp.float32)
    wire = lambda n: jax.ShapeDtypeStruct((n, rows, size), jnp.float32)
    sems = pltpu.SemaphoreType.DMA((2, 2))

    elec, magn, corr, to_core, to_chip = pl.pallas_call(
        start_kernel,
        name="start",
        out_shape=(elec_shape, magn_shape, corr_shape, wire(16), wire(16)),
        in_specs=[in_smem, in_any],
        out_specs=[in_vmem] * 5,
        scratch_shapes=[sems],
        compiler_params=params,
    )(info, fields)
    from_core, from_chip = by_core(to_core), by_chip(to_chip)
    arrived = lax.all_to_all(tensor_tiles, "space", split_axis=1, concat_axis=0, tiled=True)
    arrived = arrived.reshape(arrived.shape[0], *arrived.shape[2:])
    tensor, face_core, face_chip = pl.pallas_call(
        tensor_kernel,
        name="tensor",
        out_shape=(tensor_shape, wire(6), wire(6)),
        in_specs=[in_smem, in_smem, in_vmem, in_vmem],
        out_specs=[in_vmem] * 3,
        compiler_params=params,
    )(info, tile_index, inv_eps, arrived)
    faces = {"far": by_core(face_core), "near": by_chip(face_chip)}

    def advance(kernel, name, time_step, arrivals, fields_out=None):
        opening = time_step == 0
        closing = time_step + 2 >= steps_total
        operands = [info, ports, waves, elec, magn, tensor, corr, arrivals]
        outs = [elec_shape, magn_shape, corr_shape]
        aliases = {3: 0, 4: 1, 6: 2}
        specs = [in_smem] * 3 + [in_vmem] * 5
        out_specs = [in_vmem] * 3
        if opening:
            operands.append(faces[name])
            specs.append(in_vmem)
            outs.append(tensor_shape)
            out_specs.append(in_vmem)
            aliases[5] = 3
        if closing:
            if fields_out is not None:
                operands.append(fields_out)
                specs.append(in_any)
                aliases[8] = 3
            outs.append(whole)
            out_specs.append(in_any)
        else:
            outs.append(wire(10))
            out_specs.append(in_vmem)
        outs = pl.pallas_call(
            functools.partial(kernel, time_step, opening, closing),
            name=name,
            out_shape=tuple(outs),
            in_specs=specs,
            out_specs=out_specs,
            scratch_shapes=[sems] if closing else [],
            input_output_aliases=aliases,
            compiler_params=params,
        )(*operands)
        return outs[:3], outs[3] if opening else tensor, outs[-1]

    for time_step in range(0, steps_total, 2):
        (elec, magn, corr), tensor, to_core = advance(far_kernel, "far", time_step, from_core)
        if time_step + 2 < steps_total:
            from_core = by_core(to_core)
            (elec, magn, corr), tensor, to_chip = advance(near_kernel, "near", time_step, from_chip)
            from_chip = by_chip(to_chip)
    (elec, magn, corr), tensor, fields_out = advance(near_kernel, "near", steps_total - 2, from_chip, to_core)
    shares = lax.all_to_all(corr, "port", split_axis=0, concat_axis=0, tiled=True)
    sensitivity = pl.pallas_call(
        functools.partial(sum_kernel, 1.0 / math.sqrt(port_total * steps_total)),
        name="total",
        out_shape=jax.ShapeDtypeStruct(corr.shape[1:], jnp.float32),
        in_specs=[in_vmem],
        out_specs=in_vmem,
        compiler_params=params,
    )(shares)
    return (fields_out, sensitivity)


def solution(mesh):
    in_specs = (
        P(None, "port", None, "space", None, None),
        P(None, "space", None, None),
        P("space", None, None, None),
        P("space", None, None),
        P(),
        P(None, "port", None),
    )
    out_specs = (P(None, "port", None, "space", None, None), P("space", "port", None))
    return jax.shard_map(local, mesh=mesh, in_specs=in_specs, out_specs=out_specs, check_vma=False)
```

```python
import functools
import math

import jax
import jax.numpy as jnp
from jax import lax
from jax.experimental import pallas as pl
from jax.experimental.pallas import tpu as pltpu
from jax.sharding import PartitionSpec as P

magnetic_coef = 0.5
chunk = 8
in_vmem = pl.BlockSpec(memory_space=pltpu.VMEM)
in_smem = pl.BlockSpec(memory_space=pltpu.SMEM)
in_hbm = pl.BlockSpec(memory_space=pltpu.HBM)
params = pltpu.CompilerParams(vmem_limit_bytes=48 * 1024 * 1024)


def next_z(values, lane):
    size = values.shape[1]
    return jnp.where(lane < size - 1, pltpu.roll(values, size - 1, 1), 0.0)


def prev_z(values, lane):
    return jnp.where(lane > 0, pltpu.roll(values, 1, 1), 0.0)


class Slab:
    def __init__(self, elec, magn, tensor=None, corr=None, unroll=4):
        self.unroll = unroll
        self.elec, self.magn, self.tensor, self.corr = elec, magn, tensor, corr
        self.width_x = elec.shape[2] - 2
        self.rows = elec.shape[3] - chunk
        self.lane = lax.broadcasted_iota(jnp.int32, (chunk, elec.shape[4]), 1)

    def e(self, sim, comp, cell, y0):
        return self.elec[sim, comp, cell + 1, pl.ds(y0, chunk), :]

    def h(self, sim, comp, cell, y0):
        return self.magn[sim, comp, cell + 2, pl.ds(y0 + chunk, chunk), :]

    def put_e(self, sim, comp, cell, y0, values):
        self.elec[sim, comp, cell + 1, pl.ds(y0, chunk), :] = values

    def put_h(self, sim, comp, cell, y0, values):
        self.magn[sim, comp, cell + 2, pl.ds(y0 + chunk, chunk), :] = values

    def tensor_rows(self, cell, y0):
        first = (cell + 1) * self.rows + y0
        return pl.ds(first if isinstance(first, int) else pl.multiple_of(first, chunk), chunk)

    def tensor_at(self, cell, y0):
        spot = self.tensor_rows(cell, y0)
        return [self.tensor[i, spot, :] for i in range(6)]

    def put_tensor(self, cell, y0, entry, values):
        spot = self.tensor_rows(cell, y0)
        self.tensor[entry, spot, :] = values

    def each_chunk(self, *bodies):
        for body in bodies:

            def step(c, carry, body=body):
                for u in range(self.unroll):
                    y0 = (c * self.unroll + u) * chunk
                    body(y0 if isinstance(y0, int) else pl.multiple_of(y0, chunk))
                return carry

            trips = self.rows // (chunk * self.unroll)
            if trips == 1:
                step(0, 0)
            else:
                lax.fori_loop(0, trips, step, 0)

    def magnetic(self, cells, low_coef=magnetic_coef):
        def body(y0):
            for sim in range(2):
                for cell in cells:
                    coef = low_coef if cell == -1 else magnetic_coef
                    elec_x, elec_y, elec_z = (self.e(sim, comp, cell, y0) for comp in range(3))
                    x_up_y, z_up_y = self.e(sim, 0, cell, y0 + 1), self.e(sim, 2, cell, y0 + 1)
                    y_up_x, z_up_x = self.e(sim, 1, cell + 1, y0), self.e(sim, 2, cell + 1, y0)
                    curls = (
                        z_up_y - elec_z - (next_z(elec_y, self.lane) - elec_y),
                        next_z(elec_x, self.lane) - elec_x - (z_up_x - elec_z),
                        y_up_x - elec_y - (x_up_y - elec_x),
                    )
                    for comp, curl in enumerate(curls):
                        self.put_h(sim, comp, cell, y0, self.h(sim, comp, cell, y0) - coef * curl)

        self.each_chunk(body)

    def electric(self, cells):
        def body(y0):
            for cell in cells:
                txx, tyy, tzz, txy, txz, tyz = self.tensor_at(cell, y0)
                for sim in range(2):
                    magn_x, magn_y, magn_z = (self.h(sim, comp, cell, y0) for comp in range(3))
                    x_down_y, z_down_y = self.h(sim, 0, cell, y0 - 1), self.h(sim, 2, cell, y0 - 1)
                    y_down_x, z_down_x = self.h(sim, 1, cell - 1, y0), self.h(sim, 2, cell - 1, y0)
                    curl_x = magn_z - z_down_y - (magn_y - prev_z(magn_y, self.lane))
                    curl_y = magn_x - prev_z(magn_x, self.lane) - (magn_z - z_down_x)
                    curl_z = magn_y - y_down_x - (magn_x - x_down_y)
                    rows = ((txx, txy, txz), (txy, tyy, tyz), (txz, tyz, tzz))
                    for comp in range(1 if cell == self.width_x else 0, 3):
                        a, b, c = rows[comp]
                        change = a * curl_x + b * curl_y + c * curl_z
                        self.put_e(sim, comp, cell, y0, self.e(sim, comp, cell, y0) + change)

        self.each_chunk(body)

    def correlate(self, cells):
        def body(y0):
            for cell in cells:
                terms = [self.e(0, comp, cell, y0) * self.e(1, comp, cell, y0) for comp in range(3)]
                self.corr[y0 // chunk, cell] += terms[0] + terms[1] + terms[2]

        self.each_chunk(body)

    def sources(self, info, ports, waves, time_step, cells):
        size = self.elec.shape[4]
        plane = self.rows * size
        lane = lax.broadcasted_iota(jnp.int32, (1, size), 1)
        for sim in range(2):
            source = ports[sim, info[1]]
            cell = source // plane - info[0] * self.width_x
            rest = source % plane

            @pl.when((cell >= cells[0]) & (cell <= cells[-1]))
            def _():
                spot = (sim, 2, cell + 1, pl.ds(rest // size, 1), slice(None))
                self.elec[spot] = self.elec[spot] + jnp.where(lane == rest % size, waves[sim, 0, time_step], 0.0)

    def send_up(self, message):
        def body(y0):
            top = self.width_x - 1
            for sim in range(2):
                parts = [self.h(sim, comp, top - 1, y0) for comp in (1, 2)]
                parts += [self.e(sim, comp, top, y0) for comp in range(3)]
                for i, part in enumerate(parts):
                    message[5 * sim + i, pl.ds(y0, chunk), :] = part
                if message.shape[0] > 10:
                    for comp in range(3):
                        message[10 + 3 * sim + comp, pl.ds(y0, chunk), :] = self.h(sim, comp, top, y0)

        self.each_chunk(body)

    def send_down(self, message):
        def body(y0):
            for sim in range(2):
                parts = [self.h(sim, comp, 0, y0) for comp in range(3)] + [self.e(sim, comp, 0, y0) for comp in (1, 2)]
                for i, part in enumerate(parts):
                    message[5 * sim + i, pl.ds(y0, chunk), :] = part
                if message.shape[0] > 10:
                    for comp in range(3):
                        message[10 + 3 * sim + comp, pl.ds(y0, chunk), :] = parts[comp]

        self.each_chunk(body)

    def take_below(self, message, faces):
        def body(y0):
            spot = pl.ds(y0, chunk)
            for sim in range(2):
                for comp in (1, 2):
                    self.put_h(sim, comp, -2, y0, message[5 * sim + comp - 1, spot, :])
                for comp in range(3):
                    self.put_e(sim, comp, -1, y0, message[5 * sim + 2 + comp, spot, :])
                    if faces is not None:
                        self.put_h(sim, comp, -1, y0, message[10 + 3 * sim + comp, spot, :])
            if faces is not None:
                for entry in range(6):
                    self.put_tensor(-1, y0, entry, faces[entry, spot, :])

        self.each_chunk(body)

    def take_above(self, message, faces):
        def body(y0):
            spot = pl.ds(y0, chunk)
            for sim in range(2):
                for comp in range(3):
                    self.put_h(sim, comp, self.width_x, y0, message[5 * sim + comp, spot, :])
                for comp in (1, 2):
                    self.put_e(sim, comp, self.width_x, y0, message[5 * sim + 2 + comp, spot, :])
            if faces is not None:
                for entry in range(6):
                    self.put_tensor(self.width_x, y0, entry, faces[entry, spot, :])

        self.each_chunk(body)

    def copies_out(self, fields_out, first, count, sems):
        return [
            pltpu.make_async_copy(
                self.elec.at[sim, :, pl.ds(first + 1, count), pl.ds(0, self.rows)],
                fields_out.at[sim, 0, pl.ds(0, 3), pl.ds(first, count)],
                sems.at[sim, 0],
            )
            for sim in range(2)
        ], [
            pltpu.make_async_copy(
                self.magn.at[sim, :, pl.ds(first + 2, count), pl.ds(chunk, self.rows)],
                fields_out.at[sim, 0, pl.ds(3, 3), pl.ds(first, count)],
                sems.at[sim, 1],
            )
            for sim in range(2)
        ]


def start_kernel(info, fields, inv_eps, elec, magn, corr, tensor, to_core, to_chip, sems):
    slab = Slab(elec, magn)
    width_x, rows = slab.width_x, slab.rows
    copies = []
    for sim in range(2):
        copies.append(
            pltpu.make_async_copy(
                fields.at[sim, 0, pl.ds(0, 3)],
                elec.at[sim, :, pl.ds(1, width_x), pl.ds(0, rows)],
                sems.at[sim, 0],
            )
        )
        copies.append(
            pltpu.make_async_copy(
                fields.at[sim, 0, pl.ds(3, 3)],
                magn.at[sim, :, pl.ds(2, width_x), pl.ds(chunk, rows)],
                sems.at[sim, 1],
            )
        )
    own_rows = pl.ds(rows, width_x * rows)
    bulk = [
        pltpu.make_async_copy(
            inv_eps.at[:, x], tensor.at[pl.ds(0, 3), pl.ds((x + 1) * rows, rows)], sems.at[x % 2, 2 + x // 2]
        )
        for x in range(width_x)
    ]
    for copy in copies + bulk:
        copy.start()
    zeros = jnp.zeros((chunk, elec.shape[4]), jnp.float32)
    for sim in range(2):
        for comp in range(3):
            for x in range(elec.shape[2]):
                elec[sim, comp, x, pl.ds(rows, chunk), :] = zeros
            for x in range(magn.shape[2]):
                magn[sim, comp, x, pl.ds(0, chunk), :] = zeros
    corr[...] = jnp.zeros(corr.shape, jnp.float32)
    for entry in range(3, 6):
        tensor[entry, own_rows, :] = jnp.zeros((width_x * rows, elec.shape[4]), jnp.float32)
    for copy in copies:
        copy.wait()
    slab.magnetic((0, width_x - 2))

    @pl.when(info[2] == 0)
    def _():
        slab.send_down(to_chip)
        slab.send_up(to_core)

    @pl.when(info[2] == 1)
    def _():
        slab.send_up(to_chip)
        slab.send_down(to_core)

    for copy in bulk:
        copy.wait()


def tensor_kernel(info, index, tiles, _, tensor, to_core, to_chip):
    rows = to_core.shape[1]
    slabs, slots = index.shape[1:]
    spare = tensor.shape[1] - chunk
    width_x = spare // rows - 2

    def place(owner):
        for k in range(slots):
            column = index[0, owner, k]
            column = jnp.where(column < 0, spare, column + rows)
            for entry in range(6):
                tensor[entry, pl.ds(column, 1), :] = tiles[owner, pl.ds(6 * k + entry, 1), :]

    def some(c, carry):
        for u in range(4):
            place(4 * c + u)
        return carry

    lax.fori_loop(0, slabs // 4, some, 0)
    even = info[2] == 0
    for entry in range(6):
        first = tensor[entry, pl.ds(rows, rows), :]
        last = tensor[entry, pl.ds(width_x * rows, rows), :]
        to_core[entry] = jnp.where(even, last, first)
        to_chip[entry] = jnp.where(even, first, last)


def far_kernel(time_step, opening, closing, *refs):
    info, ports, waves, _, _, tensor, _, from_core = refs[:8]
    faces = refs[8] if opening else None
    refs = refs[9:] if opening else refs[8:]
    if closing:
        elec, magn, corr, fields_out, sems = refs
    elif opening:
        elec, magn, corr, tensor, to_core = refs
    else:
        elec, magn, corr, to_core = refs
    slab = Slab(elec, magn, tensor, corr, 8)
    top = slab.width_x

    def advance(edge, wide, own, middle, last, next_edge):
        slab.magnetic((edge, 1))
        if not opening:
            slab.correlate([cell for cell in range(top) if cell not in last])
        slab.electric(wide)
        slab.sources(info, ports, waves, time_step, wide)
        slab.correlate(own)
        slab.magnetic(middle)
        slab.electric(last)
        slab.sources(info, ports, waves, time_step + 1, last)
        slab.correlate(last)
        if not closing:
            slab.magnetic((next_edge,))

    @pl.when(info[2] == 0)
    def _():
        slab.take_above(from_core, faces)
        advance(top - 1, range(1, top + 1), range(1, top), range(1, top), range(2, top), top - 2)
        if not closing:
            slab.send_up(to_core)

    @pl.when(info[2] == 1)
    def _():
        slab.take_below(from_core, faces)
        advance(-1, range(-1, top - 1), range(top - 1), range(-1, top - 2), range(top - 2), 0)
        if not closing:
            slab.send_down(to_core)

    if closing:
        first = jnp.where(info[2] == 0, 2, 0)
        elec_copies, magn_copies = slab.copies_out(fields_out, first, 2, sems)
        for copy in elec_copies + magn_copies:
            copy.start()
        for copy in elec_copies + magn_copies:
            copy.wait()


def near_kernel(time_step, opening, closing, *refs):
    info, ports, waves, _, _, tensor, _, from_chip = refs[:8]
    faces = refs[8] if opening else None
    refs = refs[9:] if opening or closing else refs[8:]
    if closing:
        elec, magn, corr, fields_out, sems = refs
    elif opening:
        elec, magn, corr, tensor, to_chip = refs
    else:
        elec, magn, corr, to_chip = refs
    slab = Slab(elec, magn, tensor, corr, 8)
    top = slab.width_x
    low_coef = jnp.where(info[0] == 0, 0.0, magnetic_coef)

    def advance(edge, wide, own, middle, last, next_edge):
        slab.magnetic((edge,), low_coef)
        slab.electric(wide)
        slab.sources(info, ports, waves, time_step, wide)
        slab.correlate(own)
        slab.magnetic(middle, low_coef)
        if closing:
            elec_copies, magn_copies = slab.copies_out(fields_out, last[0], 2, sems)
            for copy in magn_copies:
                copy.start()
        slab.electric(last)
        slab.sources(info, ports, waves, time_step + 1, last)
        if closing:
            for copy in elec_copies:
                copy.start()
            slab.correlate(last)
            for copy in elec_copies + magn_copies:
                copy.wait()
        else:
            slab.magnetic((next_edge,))

    @pl.when(info[2] == 0)
    def _():
        slab.take_below(from_chip, faces)
        advance(-1, (-1, 0), (0,), (-1, 0), (0, 1), 0)
        if not closing:
            slab.send_down(to_chip)

    @pl.when(info[2] == 1)
    def _():
        slab.take_above(from_chip, faces)
        advance(top - 1, (top - 1, top), (top - 1,), (top - 2, top - 1), (top - 2, top - 1), top - 2)
        if not closing:
            slab.send_up(to_chip)


def sum_kernel(scale, shares, total):
    acc = shares[0]
    for i in range(1, shares.shape[0]):
        acc = acc + shares[i]
    total[...] = acc * scale


def local(fields, inv_eps, tensor_tiles, tile_index, ports, waves):
    slab_rank = lax.axis_index("space")
    port_rank = lax.axis_index("port")
    slabs = lax.axis_size("space")
    width_x, rows, size = fields.shape[3:]
    steps_total = waves.shape[2]
    port_total = ports.shape[1]
    info = jnp.stack([slab_rank, port_rank, slab_rank % 2]).astype(jnp.int32)
    core_pairs = [(i, i ^ 1) for i in range(slabs)]
    chip_pairs = [(i, ((i + 1) ^ 1) - 1) for i in range(1, slabs - 1)]

    def by_core(message):
        return lax.ppermute(message, "space", core_pairs)

    def by_chip(message):
        return lax.ppermute(message, "space", chip_pairs)

    def held(*shape):
        return pltpu.VMEM(shape, jnp.float32)

    elec_shape = held(2, 3, width_x + 2, rows + chunk, size)
    magn_shape = held(2, 3, width_x + 3, rows + chunk, size)
    corr_shape = held(rows // chunk, width_x, chunk, size)
    tensor_shape = held(6, (width_x + 2) * rows + chunk, size)
    whole = jax.ShapeDtypeStruct(fields.shape, jnp.float32)
    wire = lambda n: jax.ShapeDtypeStruct((n, rows, size), jnp.float32)
    sems = pltpu.SemaphoreType.DMA((2, 4))

    elec, magn, corr, tensor, to_core, to_chip = pl.pallas_call(
        start_kernel,
        name="start",
        out_shape=(elec_shape, magn_shape, corr_shape, tensor_shape, wire(16), wire(16)),
        in_specs=[in_smem, in_hbm, in_hbm],
        out_specs=[in_vmem] * 6,
        scratch_shapes=[sems],
        compiler_params=params,
    )(info, fields, inv_eps)
    from_core, from_chip = by_core(to_core), by_chip(to_chip)
    arrived = lax.all_to_all(tensor_tiles, "space", split_axis=1, concat_axis=0, tiled=True)
    arrived = arrived.reshape(arrived.shape[0], *arrived.shape[2:])
    tensor, face_core, face_chip = pl.pallas_call(
        tensor_kernel,
        name="tensor",
        out_shape=(tensor_shape, wire(6), wire(6)),
        in_specs=[in_smem, in_smem, in_vmem, in_vmem],
        out_specs=[in_vmem] * 3,
        input_output_aliases={3: 0},
        compiler_params=params,
    )(info, tile_index, arrived, tensor)
    faces = {"far": by_core(face_core), "near": by_chip(face_chip)}

    def advance(kernel, name, time_step, arrivals, fields_out=None):
        opening = time_step == 0
        closing = time_step + 2 >= steps_total
        operands = [info, ports, waves, elec, magn, tensor, corr, arrivals]
        outs = [elec_shape, magn_shape, corr_shape]
        aliases = {3: 0, 4: 1, 6: 2}
        specs = [in_smem] * 3 + [in_vmem] * 5
        out_specs = [in_vmem] * 3
        if opening:
            operands.append(faces[name])
            specs.append(in_vmem)
            outs.append(tensor_shape)
            out_specs.append(in_vmem)
            aliases[5] = 3
        if closing:
            if fields_out is not None:
                operands.append(fields_out)
                specs.append(in_hbm)
                aliases[8] = 3
            outs.append(whole)
            out_specs.append(in_hbm)
        else:
            outs.append(wire(10))
            out_specs.append(in_vmem)
        outs = pl.pallas_call(
            functools.partial(kernel, time_step, opening, closing),
            name=name,
            out_shape=tuple(outs),
            in_specs=specs,
            out_specs=out_specs,
            scratch_shapes=[sems] if closing else [],
            input_output_aliases=aliases,
            compiler_params=params,
        )(*operands)
        return outs[:3], outs[3] if opening else tensor, outs[-1]

    for time_step in range(0, steps_total, 2):
        (elec, magn, corr), tensor, to_core = advance(far_kernel, "far", time_step, from_core)
        if time_step + 2 < steps_total:
            from_core = by_core(to_core)
            (elec, magn, corr), tensor, to_chip = advance(near_kernel, "near", time_step, from_chip)
            from_chip = by_chip(to_chip)
    (elec, magn, corr), _, fields_out = advance(near_kernel, "near", steps_total - 2, from_chip, to_core)
    shares = lax.all_to_all(corr, "port", split_axis=0, concat_axis=0, tiled=True)
    sensitivity = pl.pallas_call(
        functools.partial(sum_kernel, 1.0 / math.sqrt(port_total * steps_total)),
        name="total",
        out_shape=jax.ShapeDtypeStruct(corr.shape[1:], jnp.float32),
        in_specs=[in_vmem],
        out_specs=in_vmem,
        compiler_params=params,
    )(shares)
    return (fields_out, sensitivity)


def solution(mesh):
    in_specs = (
        P(None, "port", None, "space", None, None),
        P(None, "space", None, None),
        P("space", None, None, None),
        P("space", None, None),
        P(),
        P(None, "port", None),
    )
    out_specs = (P(None, "port", None, "space", None, None), P("space", "port", None))
    return jax.shard_map(local, mesh=mesh, in_specs=in_specs, out_specs=out_specs, check_vma=False)
```

```python
import functools
import math

import jax
import jax.numpy as jnp
from jax import lax
from jax.experimental import pallas as pl
from jax.experimental.pallas import tpu as pltpu
from jax.sharding import PartitionSpec as P

magnetic_coef = 0.5
chunk = 8
in_vmem = pl.BlockSpec(memory_space=pltpu.VMEM)
in_smem = pl.BlockSpec(memory_space=pltpu.SMEM)
in_hbm = pl.BlockSpec(memory_space=pltpu.HBM)
params = pltpu.CompilerParams(vmem_limit_bytes=16 * 1024 * 1024)


def next_z(values, lane):
    size = values.shape[1]
    return jnp.where(lane < size - 1, pltpu.roll(values, size - 1, 1), 0.0)


def prev_z(values, lane):
    return jnp.where(lane > 0, pltpu.roll(values, 1, 1), 0.0)


class Slab:
    def __init__(self, elec, magn, tensor=None, corr=None, unroll=4):
        self.unroll = unroll
        self.base = 0
        self.elec, self.magn, self.tensor, self.corr = elec, magn, tensor, corr
        self.width_x = elec.shape[2] - 2
        self.rows = elec.shape[3] - chunk
        self.lane = lax.broadcasted_iota(jnp.int32, (chunk, elec.shape[4]), 1)

    def e(self, sim, comp, cell, y0):
        return self.elec[sim, comp, cell + 1, pl.ds(y0, chunk), :]

    def h(self, sim, comp, cell, y0):
        return self.magn[sim, comp, cell + 2, pl.ds(y0 + chunk, chunk), :]

    def put_e(self, sim, comp, cell, y0, values):
        self.elec[sim, comp, cell + 1, pl.ds(y0, chunk), :] = values

    def put_h(self, sim, comp, cell, y0, values):
        self.magn[sim, comp, cell + 2, pl.ds(y0 + chunk, chunk), :] = values

    def tensor_rows(self, cell, y0):
        first = (self.base + cell + 1) * self.rows + y0
        return pl.ds(first if isinstance(first, int) else pl.multiple_of(first, chunk), chunk)

    def tensor_at(self, cell, y0):
        spot = self.tensor_rows(cell, y0)
        return [self.tensor[i, spot, :] for i in range(6)]

    def put_tensor(self, cell, y0, entry, values):
        spot = self.tensor_rows(cell, y0)
        self.tensor[entry, spot, :] = values

    def each_chunk(self, *bodies):
        for body in bodies:

            def step(c, carry, body=body):
                for u in range(self.unroll):
                    y0 = (c * self.unroll + u) * chunk
                    body(y0 if isinstance(y0, int) else pl.multiple_of(y0, chunk))
                return carry

            trips = self.rows // (chunk * self.unroll)
            if trips == 1:
                step(0, 0)
            else:
                lax.fori_loop(0, trips, step, 0)

    def magnetic(self, cells, low_coef=magnetic_coef):
        def body(y0):
            for sim in range(2):
                for cell in cells:
                    coef = low_coef if cell == -1 else magnetic_coef
                    elec_x, elec_y, elec_z = (self.e(sim, comp, cell, y0) for comp in range(3))
                    x_up_y, z_up_y = self.e(sim, 0, cell, y0 + 1), self.e(sim, 2, cell, y0 + 1)
                    y_up_x, z_up_x = self.e(sim, 1, cell + 1, y0), self.e(sim, 2, cell + 1, y0)
                    curls = (
                        z_up_y - elec_z - (next_z(elec_y, self.lane) - elec_y),
                        next_z(elec_x, self.lane) - elec_x - (z_up_x - elec_z),
                        y_up_x - elec_y - (x_up_y - elec_x),
                    )
                    for comp, curl in enumerate(curls):
                        self.put_h(sim, comp, cell, y0, self.h(sim, comp, cell, y0) - coef * curl)

        self.each_chunk(body)

    def electric(self, cells):
        def body(y0):
            for cell in cells:
                txx, tyy, tzz, txy, txz, tyz = self.tensor_at(cell, y0)
                for sim in range(2):
                    magn_x, magn_y, magn_z = (self.h(sim, comp, cell, y0) for comp in range(3))
                    x_down_y, z_down_y = self.h(sim, 0, cell, y0 - 1), self.h(sim, 2, cell, y0 - 1)
                    y_down_x, z_down_x = self.h(sim, 1, cell - 1, y0), self.h(sim, 2, cell - 1, y0)
                    curl_x = magn_z - z_down_y - (magn_y - prev_z(magn_y, self.lane))
                    curl_y = magn_x - prev_z(magn_x, self.lane) - (magn_z - z_down_x)
                    curl_z = magn_y - y_down_x - (magn_x - x_down_y)
                    rows = ((txx, txy, txz), (txy, tyy, tyz), (txz, tyz, tzz))
                    for comp in range(1 if cell == self.width_x else 0, 3):
                        a, b, c = rows[comp]
                        change = a * curl_x + b * curl_y + c * curl_z
                        self.put_e(sim, comp, cell, y0, self.e(sim, comp, cell, y0) + change)

        self.each_chunk(body)

    def correlate(self, cells):
        def body(y0):
            for cell in cells:
                terms = [self.e(0, comp, cell, y0) * self.e(1, comp, cell, y0) for comp in range(3)]
                self.corr[y0 // chunk, cell] += terms[0] + terms[1] + terms[2]

        self.each_chunk(body)

    def sources(self, info, ports, waves, time_step, cells, slab_width=None):
        size = self.elec.shape[4]
        plane = self.rows * size
        lane = lax.broadcasted_iota(jnp.int32, (1, size), 1)
        for sim in range(2):
            source = ports[sim, info[1]]
            cell = source // plane - info[0] * (slab_width or self.width_x) - self.base
            rest = source % plane

            @pl.when((cell >= cells[0]) & (cell <= cells[-1]))
            def _():
                spot = (sim, 2, cell + 1, pl.ds(rest // size, 1), slice(None))
                self.elec[spot] = self.elec[spot] + jnp.where(lane == rest % size, waves[sim, 0, time_step], 0.0)

    def waves(self, sim, cell, y0):
        elec_x, elec_y, elec_z = (self.e(sim, comp, cell, y0) for comp in range(3))
        along_z = next_z(elec_x, self.lane) - elec_x + elec_z
        along_y = elec_y + (self.e(sim, 0, cell, y0 + 1) - elec_x)
        return along_z, along_y

    def send(self, message, first, part):
        def body(y0):
            for sim in range(2):
                for i, values in enumerate(part(sim, y0)):
                    message[first + 2 * sim + i, pl.ds(y0, chunk), :] = values

        self.each_chunk(body)

    def send_now(self, message, upward):
        top = self.width_x - 1
        self.send(
            message,
            0,
            (lambda sim, y0: self.waves(sim, top, y0))
            if upward
            else (lambda sim, y0: (self.e(sim, 1, 0, y0), self.e(sim, 2, 0, y0))),
        )

    def send_later(self, message, first, upward, scratch, info, ports, waves, time_step):
        ahead = Slab(*scratch, self.tensor, None, self.unroll)
        cell = self.width_x - 1 if upward else 0
        ahead.base = cell
        zeros = jnp.zeros((chunk, self.elec.shape[4]), jnp.float32)
        for sim in range(2):
            for comp in range(3):
                ahead.put_e(sim, comp, 0, self.rows, zeros)
                ahead.put_h(sim, comp, 0, -chunk, zeros)

        def body(y0):
            for sim in range(2):
                for comp in range(3):
                    ahead.put_e(sim, comp, 0, y0, self.e(sim, comp, cell, y0))
                    ahead.put_h(sim, comp, 0, y0, self.h(sim, comp, cell, y0))
                for comp in (1, 2):
                    ahead.put_h(sim, comp, -1, y0, self.h(sim, comp, cell - 1, y0) if upward else zeros)
                    ahead.put_e(sim, comp, 1, y0, zeros)

        self.each_chunk(body)
        if upward:
            ahead.magnetic((0,))
        ahead.electric((0,))
        ahead.sources(info, ports, waves, time_step, (0,), self.width_x)
        self.send(
            message,
            first,
            (lambda sim, y0: ahead.waves(sim, 0, y0))
            if upward
            else (lambda sim, y0: (ahead.e(sim, 1, 0, y0), ahead.e(sim, 2, 0, y0))),
        )

    def take_faces(self, cell, message):
        def body(y0):
            for entry in range(6):
                self.put_tensor(cell, y0, entry, message[4 + entry, pl.ds(y0, chunk), :])

        self.each_chunk(body)

    def take_below(self, message, opening, kept):
        def body(y0):
            spot = pl.ds(y0, chunk)
            zeros = jnp.zeros((chunk, self.elec.shape[4]), jnp.float32)
            for sim in range(2):
                for i, factor in enumerate((-magnetic_coef, magnetic_coef)):
                    old = message[4 + 2 * sim + i, spot, :] if opening else self.h(sim, i + 1, -1, y0)
                    kept[sim, i, spot, :] = old + factor * message[2 * sim + i, spot, :]
                for comp in range(3):
                    self.put_e(sim, comp, -1, y0, zeros)
                    self.put_h(sim, comp, -1, y0, zeros)

        self.each_chunk(body)

    def add_kept(self, kept):
        def body(y0):
            for sim in range(2):
                for i in range(2):
                    self.put_h(sim, i + 1, -1, y0, self.h(sim, i + 1, -1, y0) + kept[sim, i, pl.ds(y0, chunk), :])

        self.each_chunk(body)

    def add_below(self, message, first):
        def body(y0):
            for sim in range(2):
                for i, factor in enumerate((-magnetic_coef, magnetic_coef)):
                    wave = message[first + 2 * sim + i, pl.ds(y0, chunk), :]
                    self.put_h(sim, i + 1, -1, y0, self.h(sim, i + 1, -1, y0) + factor * wave)

        self.each_chunk(body)

    def take_above(self, message):
        def body(y0):
            for sim in range(2):
                for i in range(2):
                    self.put_e(sim, i + 1, self.width_x, y0, message[2 * sim + i, pl.ds(y0, chunk), :])

        self.each_chunk(body)

    def add_above(self, message, first):
        def body(y0):
            _, tyy, tzz, _, _, tyz = self.tensor_at(self.width_x, y0)
            for sim in range(2):
                magn_y, magn_z = (self.h(sim, comp, self.width_x - 1, y0) for comp in (1, 2))
                elec_y, elec_z = (message[first + 2 * sim + i, pl.ds(y0, chunk), :] for i in range(2))
                self.put_e(sim, 1, self.width_x, y0, elec_y + (tyy * magn_z - tyz * magn_y))
                self.put_e(sim, 2, self.width_x, y0, elec_z + (tyz * magn_z - tzz * magn_y))

        self.each_chunk(body)

    def copies_out(self, fields_out, first, count, sems):
        return [
            pltpu.make_async_copy(
                self.elec.at[sim, :, pl.ds(first + 1, count), pl.ds(0, self.rows)],
                fields_out.at[sim, 0, pl.ds(0, 3), pl.ds(first, count)],
                sems.at[sim, 0],
            )
            for sim in range(2)
        ], [
            pltpu.make_async_copy(
                self.magn.at[sim, :, pl.ds(first + 2, count), pl.ds(chunk, self.rows)],
                fields_out.at[sim, 0, pl.ds(3, 3), pl.ds(first, count)],
                sems.at[sim, 1],
            )
            for sim in range(2)
        ]


def start_kernel(info, fields, inv_eps, elec, magn, corr, tensor, to_core, to_chip, sems):
    slab = Slab(elec, magn)
    width_x, rows = slab.width_x, slab.rows
    copies = []
    for sim in range(2):
        copies.append(
            pltpu.make_async_copy(
                fields.at[sim, 0, pl.ds(0, 3)],
                elec.at[sim, :, pl.ds(1, width_x), pl.ds(0, rows)],
                sems.at[sim, 0],
            )
        )
        copies.append(
            pltpu.make_async_copy(
                fields.at[sim, 0, pl.ds(3, 3)],
                magn.at[sim, :, pl.ds(2, width_x), pl.ds(chunk, rows)],
                sems.at[sim, 1],
            )
        )
    own_rows = pl.ds(rows, width_x * rows)
    bulk = [
        pltpu.make_async_copy(
            inv_eps.at[:, x], tensor.at[pl.ds(0, 3), pl.ds((x + 1) * rows, rows)], sems.at[x % 2, 2 + x // 2]
        )
        for x in range(width_x)
    ]
    for copy in copies + bulk:
        copy.start()
    zeros = jnp.zeros((chunk, elec.shape[4]), jnp.float32)
    for sim in range(2):
        for comp in range(3):
            magn[sim, comp, 0] = jnp.zeros(magn.shape[3:], jnp.float32)
            for x in range(elec.shape[2]):
                elec[sim, comp, x, pl.ds(rows, chunk), :] = zeros
            for x in range(magn.shape[2]):
                magn[sim, comp, x, pl.ds(0, chunk), :] = zeros
    corr[...] = jnp.zeros(corr.shape, jnp.float32)
    for entry in range(3, 6):
        tensor[entry, own_rows, :] = jnp.zeros((width_x * rows, elec.shape[4]), jnp.float32)
    for copy in copies:
        copy.wait()
    slab.magnetic((0, width_x - 2))


    def edge_h(cell):
        return lambda sim, y0: (slab.h(sim, 1, cell, y0), slab.h(sim, 2, cell, y0))

    for parity, to_above, to_below in ((0, to_core, to_chip), (1, to_chip, to_core)):

        @pl.when(info[2] == parity)
        def _():
            slab.send_now(to_above, True)
            slab.send(to_above, 4, edge_h(width_x - 1))
            slab.send_now(to_below, False)
            slab.send(to_below, 4, edge_h(0))

    for copy in bulk:
        copy.wait()


def tensor_kernel(info, ports, waves, index, tiles, _, elec, magn, tensor, to_core, to_chip, *scratch):
    rows = to_core.shape[1]
    slabs, slots = index.shape[1:]
    spare = tensor.shape[1] - chunk
    width_x = spare // rows - 2

    def place(owner):
        for k in range(slots):
            column = index[0, owner, k]
            column = jnp.where(column < 0, spare, column + rows)
            for entry in range(6):
                tensor[entry, pl.ds(column, 1), :] = tiles[owner, pl.ds(6 * k + entry, 1), :]

    def some(c, carry):
        for u in range(4):
            place(4 * c + u)
        return carry

    lax.fori_loop(0, slabs // 4, some, 0)
    even = info[2] == 0
    for entry in range(6):
        first = tensor[entry, pl.ds(rows, rows), :]
        last = tensor[entry, pl.ds(width_x * rows, rows), :]
        to_core[4 + entry] = jnp.where(even, last, first)
        to_chip[4 + entry] = jnp.where(even, first, last)
    slab = Slab(elec, magn, tensor)
    for parity, to_above, to_below in ((0, to_core, to_chip), (1, to_chip, to_core)):

        @pl.when(info[2] == parity)
        def _():
            slab.send_later(to_above, 0, True, scratch, info, ports, waves, 0)
            slab.send_later(to_below, 0, False, scratch, info, ports, waves, 0)


def half_kernel(far, time_step, opening, closing, *refs):
    info, ports, waves, _, _, tensor, _, arrived = refs[:8]
    late, first = (refs[8], 0) if opening else (arrived, 4)
    count = 9 if opening or (closing and not far) else 8
    refs, scratch, kept = refs[count:-3], refs[-3:-1], refs[-1]
    if closing:
        elec, magn, corr, fields_out, sems = refs
    elif opening:
        elec, magn, corr, tensor, message = refs
    else:
        elec, magn, corr, message = refs
    slab = Slab(elec, magn, tensor, corr, 4 if far else 8)
    width_x = slab.width_x
    low_coef = jnp.where(info[0] == 0, 0.0, magnetic_coef)

    def advance(below, edges, wide, middle, last, next_edge):
        if opening:
            slab.take_faces(-1 if below else width_x, late)
        if below:
            slab.take_below(arrived, opening, kept)
        else:
            slab.take_above(arrived)
        slab.magnetic(edges, low_coef)
        if far and not opening:
            slab.correlate([cell for cell in range(width_x) if cell not in last])
        if below:
            slab.electric((-1,))
            slab.add_kept(kept)
        slab.electric(wide)
        if not below:
            slab.add_above(late, first)
        slab.sources(info, ports, waves, time_step, wide)
        slab.correlate(wide)
        slab.magnetic(middle, low_coef)
        if below:
            slab.add_below(late, first)
        if closing:
            elec_copies, magn_copies = slab.copies_out(fields_out, last[0], len(last), sems)
            for copy in magn_copies:
                copy.start()
        slab.electric(last)
        slab.sources(info, ports, waves, time_step + 1, last)
        if closing:
            for copy in elec_copies:
                copy.start()
        if far or closing:
            slab.correlate(last)
        if closing:
            for copy in elec_copies + magn_copies:
                copy.wait()
        else:
            slab.magnetic((next_edge,))
            slab.send_now(message, not below)
            slab.send_later(message, 4, not below, scratch, info, ports, waves, time_step + 2)

    @pl.when(info[2] == (0 if far else 1))
    def _():
        if far:
            advance(False, (width_x - 1, 1), (1, 2, 3), (1, 2, 3), (2, 3), 2)
        else:
            advance(False, (width_x - 1,), (3,), (2, 3), (2, 3), 2)

    @pl.when(info[2] == (1 if far else 0))
    def _():
        if far:
            advance(True, (-1, 1), (0, 1, 2), (-1, 0, 1), (0, 1), 0)
        else:
            advance(True, (-1,), (0,), (-1, 0), (0, 1), 0)


def sum_kernel(scale, shares, total):
    acc = shares[0]
    for i in range(1, shares.shape[0]):
        acc = acc + shares[i]
    total[...] = acc * scale


def local(fields, inv_eps, tensor_tiles, tile_index, ports, waves):
    slab_rank = lax.axis_index("space")
    port_rank = lax.axis_index("port")
    slabs = lax.axis_size("space")
    width_x, rows, size = fields.shape[3:]
    steps_total = waves.shape[2]
    port_total = ports.shape[1]
    info = jnp.stack([slab_rank, port_rank, slab_rank % 2]).astype(jnp.int32)
    core_pairs = [(i, i ^ 1) for i in range(slabs)]
    chip_pairs = [(i, ((i + 1) ^ 1) - 1) for i in range(1, slabs - 1)]

    def by_core(message):
        return lax.ppermute(message, "space", core_pairs)

    def by_chip(message):
        return lax.ppermute(message, "space", chip_pairs)

    def held(*shape):
        return pltpu.VMEM(shape, jnp.float32)

    elec_shape = held(2, 3, width_x + 2, rows + chunk, size)
    magn_shape = held(2, 3, width_x + 3, rows + chunk, size)
    corr_shape = held(rows // chunk, width_x, chunk, size)
    tensor_shape = held(6, (width_x + 2) * rows + chunk, size)
    whole = jax.ShapeDtypeStruct(fields.shape, jnp.float32)
    wire = lambda n: jax.ShapeDtypeStruct((n, rows, size), jnp.float32)
    sems = pltpu.SemaphoreType.DMA((2, 4))
    ahead_shapes = [held(2, 3, 3, rows + chunk, size), held(2, 3, 4, rows + chunk, size)]
    kept_shape = held(2, 2, rows, size)

    elec, magn, corr, tensor, to_core, to_chip = pl.pallas_call(
        start_kernel,
        name="start",
        out_shape=(elec_shape, magn_shape, corr_shape, tensor_shape, wire(8), wire(8)),
        in_specs=[in_smem, in_hbm, in_hbm],
        out_specs=[in_vmem] * 6,
        scratch_shapes=[sems],
        compiler_params=params,
    )(info, fields, inv_eps)
    from_core, from_chip = by_core(to_core), by_chip(to_chip)
    arrived = lax.all_to_all(tensor_tiles, "space", split_axis=1, concat_axis=0, tiled=True)
    arrived = arrived.reshape(arrived.shape[0], *arrived.shape[2:])
    tensor, face_core, face_chip = pl.pallas_call(
        tensor_kernel,
        name="tensor",
        out_shape=(tensor_shape, wire(10), wire(10)),
        in_specs=[in_smem] * 4 + [in_vmem] * 4,
        out_specs=[in_vmem] * 3,
        scratch_shapes=ahead_shapes,
        input_output_aliases={5: 0},
        compiler_params=params,
    )(info, ports, waves, tile_index, arrived, tensor, elec, magn)
    faces = {"far": by_core(face_core), "near": by_chip(face_chip)}

    def advance(name, time_step, arrivals, fields_out=None):
        opening = time_step == 0
        closing = time_step + 2 >= steps_total
        operands = [info, ports, waves, elec, magn, tensor, corr, arrivals]
        outs = [elec_shape, magn_shape, corr_shape]
        aliases = {3: 0, 4: 1, 6: 2}
        specs = [in_smem] * 3 + [in_vmem] * 5
        out_specs = [in_vmem] * 3
        if opening:
            operands.append(faces[name])
            specs.append(in_vmem)
            outs.append(tensor_shape)
            out_specs.append(in_vmem)
            aliases[5] = 3
        if closing:
            if fields_out is not None:
                operands.append(fields_out)
                specs.append(in_hbm)
                aliases[8] = 3
            outs.append(whole)
            out_specs.append(in_hbm)
        else:
            outs.append(wire(8))
            out_specs.append(in_vmem)
        outs = pl.pallas_call(
            functools.partial(half_kernel, name == "far", time_step, opening, closing),
            name=name,
            out_shape=tuple(outs),
            in_specs=specs,
            out_specs=out_specs,
            scratch_shapes=([sems] if closing else []) + ahead_shapes + [kept_shape],
            input_output_aliases=aliases,
            compiler_params=params,
        )(*operands)
        return outs[:3], outs[3] if opening else tensor, outs[-1]

    for time_step in range(0, steps_total, 2):
        (elec, magn, corr), tensor, to_core = advance("far", time_step, from_core)
        if time_step + 2 < steps_total:
            from_core = by_core(to_core)
            (elec, magn, corr), tensor, to_chip = advance("near", time_step, from_chip)
            from_chip = by_chip(to_chip)
    (elec, magn, corr), _, fields_out = advance("near", steps_total - 2, from_chip, to_core)
    shares = lax.all_to_all(corr, "port", split_axis=0, concat_axis=0, tiled=True)
    sensitivity = pl.pallas_call(
        functools.partial(sum_kernel, 1.0 / math.sqrt(port_total * steps_total)),
        name="total",
        out_shape=jax.ShapeDtypeStruct(corr.shape[1:], jnp.float32),
        in_specs=[in_vmem],
        out_specs=in_vmem,
        compiler_params=params,
    )(shares)
    return (fields_out, sensitivity)


def solution(mesh):
    in_specs = (
        P(None, "port", None, "space", None, None),
        P(None, "space", None, None),
        P("space", None, None, None),
        P("space", None, None),
        P(),
        P(None, "port", None),
    )
    out_specs = (P(None, "port", None, "space", None, None), P("space", "port", None))
    return jax.shard_map(local, mesh=mesh, in_specs=in_specs, out_specs=out_specs, check_vma=False)
```

```python
import functools
import math

import jax
import jax.numpy as jnp
from jax import lax
from jax.experimental import pallas as pl
from jax.experimental.pallas import tpu as pltpu
from jax.sharding import PartitionSpec as P

magnetic_coef = 0.5
chunk = 8
in_vmem = pl.BlockSpec(memory_space=pltpu.VMEM)
in_smem = pl.BlockSpec(memory_space=pltpu.SMEM)
in_any = pl.BlockSpec(memory_space=pl.ANY)
params = pltpu.CompilerParams(vmem_limit_bytes=48 * 1024 * 1024)


def next_z(values, lane):
    size = values.shape[1]
    return jnp.where(lane < size - 1, pltpu.roll(values, size - 1, 1), 0.0)


def prev_z(values, lane):
    return jnp.where(lane > 0, pltpu.roll(values, 1, 1), 0.0)


class Slab:
    def __init__(self, elec, magn, tensor=None, corr=None, unroll=4):
        self.unroll = unroll
        self.base = 0
        self.elec, self.magn, self.tensor, self.corr = elec, magn, tensor, corr
        self.width_x = elec.shape[2] - 2
        self.rows = elec.shape[3] - chunk
        self.lane = lax.broadcasted_iota(jnp.int32, (chunk, elec.shape[4]), 1)

    def e(self, sim, comp, cell, y0):
        return self.elec[sim, comp, cell + 1, pl.ds(y0, chunk), :]

    def h(self, sim, comp, cell, y0):
        return self.magn[sim, comp, cell + 2, pl.ds(y0 + chunk, chunk), :]

    def put_e(self, sim, comp, cell, y0, values):
        self.elec[sim, comp, cell + 1, pl.ds(y0, chunk), :] = values

    def put_h(self, sim, comp, cell, y0, values):
        self.magn[sim, comp, cell + 2, pl.ds(y0 + chunk, chunk), :] = values

    def tensor_rows(self, cell, y0):
        first = (self.base + cell + 1) * self.rows + y0
        return pl.ds(first if isinstance(first, int) else pl.multiple_of(first, chunk), chunk)

    def tensor_at(self, cell, y0):
        spot = self.tensor_rows(cell, y0)
        return [self.tensor[i, spot, :] for i in range(6)]

    def put_tensor(self, cell, y0, entry, values):
        spot = self.tensor_rows(cell, y0)
        self.tensor[entry, spot, :] = values

    def each_chunk(self, *bodies):
        for body in bodies:

            def step(c, carry, body=body):
                for u in range(self.unroll):
                    y0 = (c * self.unroll + u) * chunk
                    body(y0 if isinstance(y0, int) else pl.multiple_of(y0, chunk))
                return carry

            trips = self.rows // (chunk * self.unroll)
            if trips == 1:
                step(0, 0)
            else:
                lax.fori_loop(0, trips, step, 0)

    def magnetic(self, cells, low_coef=magnetic_coef):
        def body(y0):
            for sim in range(2):
                for cell in cells:
                    coef = low_coef if cell == -1 else magnetic_coef
                    elec_x, elec_y, elec_z = (self.e(sim, comp, cell, y0) for comp in range(3))
                    x_up_y, z_up_y = self.e(sim, 0, cell, y0 + 1), self.e(sim, 2, cell, y0 + 1)
                    y_up_x, z_up_x = self.e(sim, 1, cell + 1, y0), self.e(sim, 2, cell + 1, y0)
                    curls = (
                        z_up_y - elec_z - (next_z(elec_y, self.lane) - elec_y),
                        next_z(elec_x, self.lane) - elec_x - (z_up_x - elec_z),
                        y_up_x - elec_y - (x_up_y - elec_x),
                    )
                    for comp, curl in enumerate(curls):
                        self.put_h(sim, comp, cell, y0, self.h(sim, comp, cell, y0) - coef * curl)

        self.each_chunk(body)

    def electric(self, cells):
        def body(y0):
            for cell in cells:
                txx, tyy, tzz, txy, txz, tyz = self.tensor_at(cell, y0)
                for sim in range(2):
                    magn_x, magn_y, magn_z = (self.h(sim, comp, cell, y0) for comp in range(3))
                    x_down_y, z_down_y = self.h(sim, 0, cell, y0 - 1), self.h(sim, 2, cell, y0 - 1)
                    y_down_x, z_down_x = self.h(sim, 1, cell - 1, y0), self.h(sim, 2, cell - 1, y0)
                    curl_x = magn_z - z_down_y - (magn_y - prev_z(magn_y, self.lane))
                    curl_y = magn_x - prev_z(magn_x, self.lane) - (magn_z - z_down_x)
                    curl_z = magn_y - y_down_x - (magn_x - x_down_y)
                    rows = ((txx, txy, txz), (txy, tyy, tyz), (txz, tyz, tzz))
                    for comp in range(1 if cell == self.width_x else 0, 3):
                        a, b, c = rows[comp]
                        change = a * curl_x + b * curl_y + c * curl_z
                        self.put_e(sim, comp, cell, y0, self.e(sim, comp, cell, y0) + change)

        self.each_chunk(body)

    def correlate(self, cells):
        def body(y0):
            for cell in cells:
                terms = [self.e(0, comp, cell, y0) * self.e(1, comp, cell, y0) for comp in range(3)]
                self.corr[y0 // chunk, cell] += terms[0] + terms[1] + terms[2]

        self.each_chunk(body)

    def sources(self, info, ports, waves, time_step, cells, slab_width=None):
        size = self.elec.shape[4]
        plane = self.rows * size
        lane = lax.broadcasted_iota(jnp.int32, (1, size), 1)
        for sim in range(2):
            source = ports[sim, info[1]]
            cell = source // plane - info[0] * (slab_width or self.width_x) - self.base
            rest = source % plane

            @pl.when((cell >= cells[0]) & (cell <= cells[-1]))
            def _():
                spot = (sim, 2, cell + 1, pl.ds(rest // size, 1), slice(None))
                self.elec[spot] = self.elec[spot] + jnp.where(lane == rest % size, waves[sim, 0, time_step], 0.0)

    def waves(self, sim, cell, y0):
        elec_x, elec_y, elec_z = (self.e(sim, comp, cell, y0) for comp in range(3))
        along_z = next_z(elec_x, self.lane) - elec_x + elec_z
        along_y = elec_y + (self.e(sim, 0, cell, y0 + 1) - elec_x)
        return along_z, along_y

    def send(self, message, first, part):
        def body(y0):
            for sim in range(2):
                for i, values in enumerate(part(sim, y0)):
                    message[first + 2 * sim + i, pl.ds(y0, chunk), :] = values

        self.each_chunk(body)

    def send_now(self, message, upward):
        top = self.width_x - 1
        self.send(
            message,
            0,
            (lambda sim, y0: self.waves(sim, top, y0))
            if upward
            else (lambda sim, y0: (self.e(sim, 1, 0, y0), self.e(sim, 2, 0, y0))),
        )

    def send_later(self, message, first, upward, scratch, info, ports, waves, time_step):
        ahead = Slab(*scratch, self.tensor, None, self.unroll)
        cell = self.width_x - 1 if upward else 0
        ahead.base = cell
        zeros = jnp.zeros((chunk, self.elec.shape[4]), jnp.float32)
        for sim in range(2):
            for comp in range(3):
                ahead.put_e(sim, comp, 0, self.rows, zeros)
                ahead.put_h(sim, comp, 0, -chunk, zeros)

        def body(y0):
            for sim in range(2):
                for comp in range(3):
                    ahead.put_e(sim, comp, 0, y0, self.e(sim, comp, cell, y0))
                    ahead.put_h(sim, comp, 0, y0, self.h(sim, comp, cell, y0))
                for comp in (1, 2):
                    ahead.put_h(sim, comp, -1, y0, self.h(sim, comp, cell - 1, y0) if upward else zeros)
                    ahead.put_e(sim, comp, 1, y0, zeros)

        self.each_chunk(body)
        if upward:
            ahead.magnetic((0,))
        ahead.electric((0,))
        ahead.sources(info, ports, waves, time_step, (0,), self.width_x)
        self.send(
            message,
            first,
            (lambda sim, y0: ahead.waves(sim, 0, y0))
            if upward
            else (lambda sim, y0: (ahead.e(sim, 1, 0, y0), ahead.e(sim, 2, 0, y0))),
        )

    def take_below(self, message, kept):
        def body(y0):
            spot = pl.ds(y0, chunk)
            zeros = jnp.zeros((chunk, self.elec.shape[4]), jnp.float32)
            for sim in range(2):
                for i, factor in enumerate((-magnetic_coef, magnetic_coef)):
                    kept[sim, i, spot, :] = self.h(sim, i + 1, -1, y0) + factor * message[2 * sim + i, spot, :]
                    self.put_h(sim, i + 1, -2, y0, zeros)
                for comp in range(3):
                    self.put_e(sim, comp, -1, y0, zeros)
                    self.put_h(sim, comp, -1, y0, zeros)

        self.each_chunk(body)

    def add_kept(self, kept):
        def body(y0):
            for sim in range(2):
                for i in range(2):
                    self.put_h(sim, i + 1, -1, y0, self.h(sim, i + 1, -1, y0) + kept[sim, i, pl.ds(y0, chunk), :])

        self.each_chunk(body)

    def add_below(self, message, first):
        def body(y0):
            for sim in range(2):
                for i, factor in enumerate((-magnetic_coef, magnetic_coef)):
                    wave = message[first + 2 * sim + i, pl.ds(y0, chunk), :]
                    self.put_h(sim, i + 1, -1, y0, self.h(sim, i + 1, -1, y0) + factor * wave)

        self.each_chunk(body)

    def take_above(self, message):
        def body(y0):
            for sim in range(2):
                for i in range(2):
                    self.put_e(sim, i + 1, self.width_x, y0, message[2 * sim + i, pl.ds(y0, chunk), :])

        self.each_chunk(body)

    def add_above(self, message, first):
        def body(y0):
            _, tyy, tzz, _, _, tyz = self.tensor_at(self.width_x, y0)
            for sim in range(2):
                magn_y, magn_z = (self.h(sim, comp, self.width_x - 1, y0) for comp in (1, 2))
                elec_y, elec_z = (message[first + 2 * sim + i, pl.ds(y0, chunk), :] for i in range(2))
                self.put_e(sim, 1, self.width_x, y0, elec_y + (tyy * magn_z - tyz * magn_y))
                self.put_e(sim, 2, self.width_x, y0, elec_z + (tyz * magn_z - tzz * magn_y))

        self.each_chunk(body)

    def open_up(self, message):
        def body(y0):
            top = self.width_x - 1
            for sim in range(2):
                parts = [self.h(sim, comp, top - 1, y0) for comp in (1, 2)]
                parts += [self.e(sim, comp, top, y0) for comp in range(3)]
                for i, part in enumerate(parts):
                    message[5 * sim + i, pl.ds(y0, chunk), :] = part
                if message.shape[0] > 10:
                    for comp in range(3):
                        message[10 + 3 * sim + comp, pl.ds(y0, chunk), :] = self.h(sim, comp, top, y0)

        self.each_chunk(body)

    def open_down(self, message):
        def body(y0):
            for sim in range(2):
                parts = [self.h(sim, comp, 0, y0) for comp in range(3)] + [self.e(sim, comp, 0, y0) for comp in (1, 2)]
                for i, part in enumerate(parts):
                    message[5 * sim + i, pl.ds(y0, chunk), :] = part
                if message.shape[0] > 10:
                    for comp in range(3):
                        message[10 + 3 * sim + comp, pl.ds(y0, chunk), :] = parts[comp]

        self.each_chunk(body)

    def open_below(self, message, faces):
        def body(y0):
            spot = pl.ds(y0, chunk)
            for sim in range(2):
                for comp in (1, 2):
                    self.put_h(sim, comp, -2, y0, message[5 * sim + comp - 1, spot, :])
                for comp in range(3):
                    self.put_e(sim, comp, -1, y0, message[5 * sim + 2 + comp, spot, :])
                    if faces is not None:
                        self.put_h(sim, comp, -1, y0, message[10 + 3 * sim + comp, spot, :])
            if faces is not None:
                for entry in range(6):
                    self.put_tensor(-1, y0, entry, faces[entry, spot, :])

        self.each_chunk(body)

    def open_above(self, message, faces):
        def body(y0):
            spot = pl.ds(y0, chunk)
            for sim in range(2):
                for comp in range(3):
                    self.put_h(sim, comp, self.width_x, y0, message[5 * sim + comp, spot, :])
                for comp in (1, 2):
                    self.put_e(sim, comp, self.width_x, y0, message[5 * sim + 2 + comp, spot, :])
            if faces is not None:
                for entry in range(6):
                    self.put_tensor(self.width_x, y0, entry, faces[entry, spot, :])

        self.each_chunk(body)

    def copies_out(self, fields_out, first, count, sems):
        return [
            pltpu.make_async_copy(
                self.elec.at[sim, :, pl.ds(first + 1, count), pl.ds(0, self.rows)],
                fields_out.at[sim, 0, pl.ds(0, 3), pl.ds(first, count)],
                sems.at[sim, 0],
            )
            for sim in range(2)
        ], [
            pltpu.make_async_copy(
                self.magn.at[sim, :, pl.ds(first + 2, count), pl.ds(chunk, self.rows)],
                fields_out.at[sim, 0, pl.ds(3, 3), pl.ds(first, count)],
                sems.at[sim, 1],
            )
            for sim in range(2)
        ]


def start_kernel(info, fields, elec, magn, corr, to_core, to_chip, sems):
    slab = Slab(elec, magn)
    width_x, rows = slab.width_x, slab.rows
    copies = []
    for sim in range(2):
        copies.append(
            pltpu.make_async_copy(
                fields.at[sim, 0, pl.ds(0, 3)],
                elec.at[sim, :, pl.ds(1, width_x), pl.ds(0, rows)],
                sems.at[sim, 0],
            )
        )
        copies.append(
            pltpu.make_async_copy(
                fields.at[sim, 0, pl.ds(3, 3)],
                magn.at[sim, :, pl.ds(2, width_x), pl.ds(chunk, rows)],
                sems.at[sim, 1],
            )
        )
    for copy in copies:
        copy.start()
    zeros = jnp.zeros((chunk, elec.shape[4]), jnp.float32)
    for sim in range(2):
        for comp in range(3):
            for x in range(elec.shape[2]):
                elec[sim, comp, x, pl.ds(rows, chunk), :] = zeros
            for x in range(magn.shape[2]):
                magn[sim, comp, x, pl.ds(0, chunk), :] = zeros
    corr[...] = jnp.zeros(corr.shape, jnp.float32)
    for copy in copies:
        copy.wait()
    slab.magnetic((0, width_x - 2))

    @pl.when(info[2] == 0)
    def _():
        slab.open_down(to_chip)
        slab.open_up(to_core)

    @pl.when(info[2] == 1)
    def _():
        slab.open_up(to_chip)
        slab.open_down(to_core)


def tensor_kernel(info, index, inv_eps, tiles, tensor, to_core, to_chip):
    width_x, rows, size = inv_eps.shape[1:]
    slabs, slots = index.shape[1:]
    spare = (width_x + 2) * rows
    zeros = jnp.zeros((chunk, size), jnp.float32)

    def fill(c, carry):
        y0 = pl.multiple_of(c * chunk, chunk)
        for comp in range(3):
            for x in range(width_x):
                spot = pl.ds(pl.multiple_of((x + 1) * rows + y0, chunk), chunk)
                tensor[comp, spot, :] = inv_eps[comp, x, pl.ds(y0, chunk), :]
                tensor[comp + 3, spot, :] = zeros
        return carry

    lax.fori_loop(0, rows // chunk, fill, 0)

    def place(owner, carry):
        for k in range(slots):
            column = index[0, owner, k]
            column = jnp.where(column < 0, spare, column + rows)
            for entry in range(6):
                tensor[entry, pl.ds(column, 1), :] = tiles[owner, pl.ds(6 * k + entry, 1), :]
        return carry

    lax.fori_loop(0, slabs, place, 0)
    even = info[2] == 0
    for entry in range(6):
        first = tensor[entry, pl.ds(rows, rows), :]
        last = tensor[entry, pl.ds(width_x * rows, rows), :]
        to_core[entry] = jnp.where(even, last, first)
        to_chip[entry] = jnp.where(even, first, last)


def half_kernel(far, time_step, opening, closing, *refs):
    info, ports, waves, _, _, tensor, _, arrived = refs[:8]
    faces = refs[8] if opening else None
    count = 9 if opening or (closing and not far) else 8
    refs, scratch, kept = refs[count:-3], refs[-3:-1], refs[-1]
    if closing:
        elec, magn, corr, fields_out, sems = refs
    elif opening:
        elec, magn, corr, tensor, message = refs
    else:
        elec, magn, corr, message = refs
    slab = Slab(elec, magn, tensor, corr, 4 if far else 8)
    width_x = slab.width_x
    low_coef = jnp.where(info[0] == 0, 0.0, magnetic_coef)

    def advance(below, edges, wide, middle, last, next_edge):
        ghost = (-1,) if below else (width_x,)
        if opening and below:
            slab.open_below(arrived, faces)
        elif opening:
            slab.open_above(arrived, faces)
        elif below:
            slab.take_below(arrived, kept)
        else:
            slab.take_above(arrived)
        slab.magnetic(edges, low_coef)
        if far and not opening:
            slab.correlate([cell for cell in range(width_x) if cell not in last])
        if opening:
            reached = ghost + wide if below else wide + ghost
            slab.electric(reached)
            slab.sources(info, ports, waves, time_step, reached)
        else:
            if below:
                slab.electric(ghost)
                slab.add_kept(kept)
            slab.electric(wide)
            if not below:
                slab.add_above(arrived, 4)
            slab.sources(info, ports, waves, time_step, wide)
        slab.correlate(wide)
        slab.magnetic(middle, low_coef)
        if below and not opening:
            slab.add_below(arrived, 4)
        if closing:
            elec_copies, magn_copies = slab.copies_out(fields_out, last[0], len(last), sems)
            for copy in magn_copies:
                copy.start()
        slab.electric(last)
        slab.sources(info, ports, waves, time_step + 1, last)
        if closing:
            for copy in elec_copies:
                copy.start()
        if far or closing:
            slab.correlate(last)
        if closing:
            for copy in elec_copies + magn_copies:
                copy.wait()
        else:
            slab.magnetic((next_edge,))
            slab.send_now(message, not below)
            slab.send_later(message, 4, not below, scratch, info, ports, waves, time_step + 2)

    @pl.when(info[2] == (0 if far else 1))
    def _():
        if far:
            advance(False, (width_x - 1, 1), (1, 2, 3), (1, 2, 3), (2, 3), 2)
        else:
            advance(False, (width_x - 1,), (3,), (2, 3), (2, 3), 2)

    @pl.when(info[2] == (1 if far else 0))
    def _():
        if far:
            advance(True, (-1, 1), (0, 1, 2), (-1, 0, 1), (0, 1), 0)
        else:
            advance(True, (-1,), (0,), (-1, 0), (0, 1), 0)


def sum_kernel(scale, shares, total):
    acc = shares[0]
    for i in range(1, shares.shape[0]):
        acc = acc + shares[i]
    total[...] = acc * scale


def local(fields, inv_eps, tensor_tiles, tile_index, ports, waves):
    slab_rank = lax.axis_index("space")
    port_rank = lax.axis_index("port")
    slabs = lax.axis_size("space")
    width_x, rows, size = fields.shape[3:]
    steps_total = waves.shape[2]
    port_total = ports.shape[1]
    info = jnp.stack([slab_rank, port_rank, slab_rank % 2]).astype(jnp.int32)
    core_pairs = [(i, i ^ 1) for i in range(slabs)]
    chip_pairs = [(i, ((i + 1) ^ 1) - 1) for i in range(1, slabs - 1)]

    def by_core(message):
        return lax.ppermute(message, "space", core_pairs)

    def by_chip(message):
        return lax.ppermute(message, "space", chip_pairs)

    def held(*shape):
        return pltpu.VMEM(shape, jnp.float32)

    elec_shape = held(2, 3, width_x + 2, rows + chunk, size)
    magn_shape = held(2, 3, width_x + 3, rows + chunk, size)
    corr_shape = held(rows // chunk, width_x, chunk, size)
    tensor_shape = held(6, (width_x + 2) * rows + chunk, size)
    whole = jax.ShapeDtypeStruct(fields.shape, jnp.float32)
    wire = lambda n: jax.ShapeDtypeStruct((n, rows, size), jnp.float32)
    sems = pltpu.SemaphoreType.DMA((2, 2))
    ahead_shapes = [held(2, 3, 3, rows + chunk, size), held(2, 3, 4, rows + chunk, size)]
    kept_shape = held(2, 2, rows, size)

    elec, magn, corr, to_core, to_chip = pl.pallas_call(
        start_kernel,
        name="start",
        out_shape=(elec_shape, magn_shape, corr_shape, wire(16), wire(16)),
        in_specs=[in_smem, in_any],
        out_specs=[in_vmem] * 5,
        scratch_shapes=[sems],
        compiler_params=params,
    )(info, fields)
    from_core, from_chip = by_core(to_core), by_chip(to_chip)
    arrived = lax.all_to_all(tensor_tiles, "space", split_axis=1, concat_axis=0, tiled=True)
    arrived = arrived.reshape(arrived.shape[0], *arrived.shape[2:])
    tensor, face_core, face_chip = pl.pallas_call(
        tensor_kernel,
        name="tensor",
        out_shape=(tensor_shape, wire(6), wire(6)),
        in_specs=[in_smem, in_smem, in_vmem, in_vmem],
        out_specs=[in_vmem] * 3,
        compiler_params=params,
    )(info, tile_index, inv_eps, arrived)
    faces = {"far": by_core(face_core), "near": by_chip(face_chip)}

    def advance(name, time_step, arrivals, fields_out=None):
        opening = time_step == 0
        closing = time_step + 2 >= steps_total
        operands = [info, ports, waves, elec, magn, tensor, corr, arrivals]
        outs = [elec_shape, magn_shape, corr_shape]
        aliases = {3: 0, 4: 1, 6: 2}
        specs = [in_smem] * 3 + [in_vmem] * 5
        out_specs = [in_vmem] * 3
        if opening:
            operands.append(faces[name])
            specs.append(in_vmem)
            outs.append(tensor_shape)
            out_specs.append(in_vmem)
            aliases[5] = 3
        if closing:
            if fields_out is not None:
                operands.append(fields_out)
                specs.append(in_any)
                aliases[8] = 3
            outs.append(whole)
            out_specs.append(in_any)
        else:
            outs.append(wire(8))
            out_specs.append(in_vmem)
        outs = pl.pallas_call(
            functools.partial(half_kernel, name == "far", time_step, opening, closing),
            name=name,
            out_shape=tuple(outs),
            in_specs=specs,
            out_specs=out_specs,
            scratch_shapes=([sems] if closing else []) + ahead_shapes + [kept_shape],
            input_output_aliases=aliases,
            compiler_params=params,
        )(*operands)
        return outs[:3], outs[3] if opening else tensor, outs[-1]

    for time_step in range(0, steps_total, 2):
        (elec, magn, corr), tensor, to_core = advance("far", time_step, from_core)
        if time_step + 2 < steps_total:
            from_core = by_core(to_core)
            (elec, magn, corr), tensor, to_chip = advance("near", time_step, from_chip)
            from_chip = by_chip(to_chip)
    (elec, magn, corr), _, fields_out = advance("near", steps_total - 2, from_chip, to_core)
    shares = lax.all_to_all(corr, "port", split_axis=0, concat_axis=0, tiled=True)
    sensitivity = pl.pallas_call(
        functools.partial(sum_kernel, 1.0 / math.sqrt(port_total * steps_total)),
        name="total",
        out_shape=jax.ShapeDtypeStruct(corr.shape[1:], jnp.float32),
        in_specs=[in_vmem],
        out_specs=in_vmem,
        compiler_params=params,
    )(shares)
    return (fields_out, sensitivity)


def solution(mesh):
    in_specs = (
        P(None, "port", None, "space", None, None),
        P(None, "space", None, None),
        P("space", None, None, None),
        P("space", None, None),
        P(),
        P(None, "port", None),
    )
    out_specs = (P(None, "port", None, "space", None, None), P("space", "port", None))
    return jax.shard_map(local, mesh=mesh, in_specs=in_specs, out_specs=out_specs, check_vma=False)
```
